32 devices in a mesh: groups: 1, row: 32 (over z, y, x, core), col: 1.
Axes of the slice: x: 2, y: 2, z: 4, core: 2. Of those that a mesh axis runs over, the one named last changes fastest.
Arguments:
- features_in: bfloat16 [64, 128, 128], P(None, ('groups', 'row'), 'col'), may hold values from -6 to 6
- gain_outer: float32 [8, 64], replicated, may hold values from 0.25 to 1.75
- bias_outer: float32 [8, 64], replicated, may hold values from -3 to 3
- w_narrow: bfloat16 [8, 32, 576], replicated, may hold values from -0.25 to 0.25
- gain_inner: float32 [8, 32], replicated, may hold values from 0.25 to 1.75
- bias_inner: float32 [8, 32], replicated, may hold values from -3 to 3
- w_widen: bfloat16 [8, 64, 288], replicated, may hold values from -0.375 to 0.375
Outputs:
- features_out: bfloat16 [64, 128, 128], P(None, ('groups', 'row'), 'col')
The draws below stay inside these ranges and needn't reach their ends.
All inputs are finite; a program needn't handle non-finite values.
Results may differ from the reference program's by a relative error of at most 0.022.
Values may be sent and summed in bfloat16 or wider, within the bound.
A program may use at most 64 MiB of HBM per device.

```python
import jax
import jax.numpy as jnp
from jax import lax

CH = 64
MID = 32
ROUNDS = 2
BLOCKS = 8
L = 128


def steps_of(stream_key, extent, shards, smallest, top_value):
    factor_of = 1.0
    for dim, parts in shards:
        heights = jax.random.uniform(jax.random.fold_in(jax.random.fold_in(stream_key, 6), dim), (parts,), jnp.float32, smallest / len(shards), top_value / len(shards))
        factor_of = factor_of * jnp.repeat(jnp.exp(heights), extent[dim] // parts).reshape((-1,) + (1,) * (len(extent) - 1 - dim))
    return factor_of


def noise(own_key, dims, scale, reach, split=(), held_as=jnp.bfloat16):
    factor_of = steps_of(own_key, dims, split, -0.22, 0.18) if split else 1.0
    array = jax.random.normal(own_key, dims, jnp.float32) * scale * factor_of
    return jnp.minimum(jnp.maximum(array, -reach), reach).astype(held_as)


def setup_inputs(seed: int = 0, part: int = 0) -> dict:
    arg_keys = jax.random.split(jax.random.key(seed), 8)
    own_keys = jax.random.split(jax.random.fold_in(arg_keys[7], part), 8)
    features_in = noise(own_keys[0], (CH, L, L), 1.0, 6.0, ((1, 32),))
    gain_outer = jnp.clip(1.0 + 0.15 * jax.random.normal(arg_keys[1], (BLOCKS, CH), jnp.float32), 0.25, 1.75)
    bias_outer = noise(arg_keys[2], (BLOCKS, CH), 0.5, 3.0, (), jnp.float32)
    w_narrow = noise(arg_keys[3], (BLOCKS, MID, 9 * CH), (9 * CH) ** -0.5, 0.25)
    gain_inner = jnp.clip(1.0 + 0.15 * jax.random.normal(arg_keys[4], (BLOCKS, MID), jnp.float32), 0.25, 1.75)
    bias_inner = noise(arg_keys[5], (BLOCKS, MID), 0.5, 3.0, (), jnp.float32)
    w_widen = noise(arg_keys[6], (BLOCKS, CH, 9 * MID), (9 * MID) ** -0.5, 0.375)
    return {"features_in": features_in, "gain_outer": gain_outer, "bias_outer": bias_outer, "w_narrow": w_narrow, "gain_inner": gain_inner, "bias_inner": bias_inner, "w_widen": w_widen}


def dilated_conv(hidden, weight, dilation):
    out_count = weight.shape[0]
    in_count = hidden.shape[0]
    kernel = weight.astype(jnp.float32).reshape(out_count, 3, 3, in_count).transpose(0, 3, 1, 2)
    result = lax.conv_general_dilated(hidden[None], kernel, (1, 1), ((dilation, dilation), (dilation, dilation)), rhs_dilation=(dilation, dilation), dimension_numbers=("NCHW", "OIHW", "NCHW"), precision=lax.Precision.HIGHEST)
    return result[0]


def reference(features_in, gain_outer, bias_outer, w_narrow, gain_inner, bias_inner, w_widen):
    stream = features_in
    for repeat in range(ROUNDS):
        stream_f = stream.astype(jnp.float32)
        stream = ((stream_f + jnp.transpose(stream_f, (0, 2, 1))) * 0.5).astype(jnp.bfloat16)
        for within in range(4):
            block = repeat * 4 + within
            dilation = 1 + within // 2
            stream_f = stream.astype(jnp.float32)
            hidden = jax.nn.relu(stream_f * gain_outer[block][:, None, None] + bias_outer[block][:, None, None]).astype(jnp.bfloat16)
            hidden = lax.optimization_barrier(hidden).astype(jnp.float32)
            narrow = dilated_conv(hidden, w_narrow[block], dilation)
            inner = jax.nn.relu(narrow * gain_inner[block][:, None, None] + bias_inner[block][:, None, None]).astype(jnp.bfloat16)
            inner = lax.optimization_barrier(inner).astype(jnp.float32)
            widened = dilated_conv(inner, w_widen[block], dilation)
            stream = (stream_f + widened).astype(jnp.bfloat16)
    return stream
```

```python
import functools

import numpy as np
import jax
import jax.numpy as jnp
from jax import lax
from jax.experimental import pallas as pl
from jax.experimental.pallas import tpu as pltpu
from jax.sharding import PartitionSpec as P

GROUPS = ((1, 1), (2, 2))
LANES = 128


def remote(src, dst, send_sem, recv_sem, target):
    return pltpu.make_async_remote_copy(
        src_ref=src,
        dst_ref=dst,
        send_sem=send_sem,
        recv_sem=recv_sem,
        device_id={"row": target},
        device_id_type=pl.DeviceIdType.MESH,
    )


def spread_constants(rows, channels, width):
    count = width // rows
    halves = rows * channels // LANES
    pieces = rows * halves
    subs = LANES // channels
    p = np.arange(width * halves)
    pack = np.zeros((width * halves, halves * width), np.float32)
    pack[p, (p % halves) * width + p // halves] = 1
    o = np.arange(rows * width)
    xx, x = o // width, o % width
    j, r = x // rows, x % rows
    q = (r % subs) * (count * pieces) + j * pieces + xx * halves + r // subs
    unpack = np.zeros((subs * count * pieces, rows * width), np.float32)
    unpack[q, o] = 1
    return jnp.asarray(pack, jnp.bfloat16), jnp.asarray(unpack, jnp.bfloat16)


def shifted_sum(parts, dilation, lane):
    width = lane.shape[-1]
    low = jnp.where(lane < dilation, 0.0, pltpu.roll(parts[0], dilation, 1))
    high = jnp.where(lane >= width - dilation, 0.0, pltpu.roll(parts[2], width - dilation, 1))
    return parts[1] + low + high


def network_kernel(
    count, rounds, x_ref, params_ref, wn_ref, ww_ref, pack_ref, unpack_ref, out_ref, *scratch
):
    rows, channels, width = x_ref.shape
    mid = ww_ref.shape[2] // 3
    side = rows * count
    halves = rows * channels // LANES
    subs = LANES // channels
    pieces = rows * halves
    groups = len(GROUPS)
    tiles = scratch[: rounds * groups]
    sent, got, stream_buf, hidden_buf, inner_buf = scratch[rounds * groups : rounds * groups + 5]
    mirror_send, mirror_recv, halo_send, halo_recv = scratch[rounds * groups + 5 :]
    me = lax.axis_index("row")

    barrier = pltpu.get_barrier_semaphore()

    def greet(k, carry):
        pl.semaphore_signal(
            barrier,
            inc=1,
            device_id={"row": lax.rem(me + k, count)},
            device_id_type=pl.DeviceIdType.MESH,
        )
        return carry

    lax.fori_loop(1, count, greet, 0)
    for phase in range(rounds * groups):
        tile = tiles[phase]
        reach = tile.shape[0] // 2
        for k in range(1, reach + 1):
            for sign in (-1, 1):
                slot = reach + sign * k
                other = me + sign * k

                @pl.when((other < 0) | (other >= count))
                def _():
                    tile[slot] = jnp.zeros(tile.shape[1:], tile.dtype)

    def pack(rd, stream):
        flat = [s for s in stream]
        per = LANES // channels
        cat = jnp.concatenate(
            [jnp.concatenate(flat[h * per : (h + 1) * per], axis=0) for h in range(halves)], axis=1
        )
        packed = lax.dot_general(
            pack_ref[...], cat, (((1,), (1,)), ((), ())), preferred_element_type=jnp.float32
        )
        sent[rd] = packed.reshape(count, pieces, LANES).astype(jnp.bfloat16)

    def mirror_copy(rd, target, source):
        return remote(
            sent.at[rd, target],
            got.at[rd, source],
            mirror_send.at[rd, target],
            mirror_recv.at[rd, source],
            target,
        )

    lane = lax.broadcasted_iota(jnp.int32, (1, width), 1)
    stream = [x_ref[r] for r in range(rows)]
    pack(0, stream)
    pl.semaphore_wait(barrier, count - 1)

    for rd in range(rounds):
        if rd:
            pack(rd, stream)

        def send(k, carry):
            mirror_copy(rd, lax.rem(me + k, count), me).start()
            return carry

        def receive(k, carry):
            source = lax.rem(me + k, count)
            mirror_copy(rd, source, source).wait_recv()
            return carry

        lax.fori_loop(1, count, send, 0)
        got[rd, me] = sent[rd, me]
        lax.fori_loop(1, count, receive, 0)

        arrived = got[rd].astype(jnp.float32).reshape(count * pieces, LANES).T
        arrived = jnp.concatenate(
            [arrived[u * channels : (u + 1) * channels] for u in range(subs)], axis=1
        ).astype(jnp.bfloat16)
        partner = jnp.dot(arrived, unpack_ref[...], preferred_element_type=jnp.float32)
        stream = [
            (
                (stream[r].astype(jnp.float32) + partner[:, r * width : (r + 1) * width]) * 0.5
            ).astype(jnp.bfloat16)
            for r in range(rows)
        ]

        block = rd * sum(len(g) for g in GROUPS)
        for gi, group in enumerate(GROUPS):
            phase = rd * groups + gi
            tile = tiles[phase]
            reach = tile.shape[0] // 2
            for r in range(rows):
                tile[reach, r] = stream[r]

            def halo_copy(k, slot_there, target):
                return remote(
                    tile.at[reach],
                    tile.at[slot_there],
                    halo_send.at[phase, reach + k],
                    halo_recv.at[phase, slot_there],
                    target,
                )

            offsets = [s * k for k in range(1, reach + 1) for s in (-1, 1)]
            for k in offsets:

                @pl.when((me + k >= 0) & (me + k < count))
                def _():
                    halo_copy(k, reach - k, me + k).start()

            for k in offsets:

                @pl.when((me + k >= 0) & (me + k < count))
                def _():
                    halo_copy(k, reach + k, me + k).wait_recv()

            halo = 2 * sum(group)
            lo = reach * rows - halo
            hi = (reach + 1) * rows + halo
            first_row = (me - reach) * rows

            def inside(e):
                g = first_row + e
                return jnp.where((g >= 0) & (g < side), 1.0, 0.0).astype(jnp.float32)

            def masked(value, e):
                if reach * rows <= e < (reach + 1) * rows:
                    return value
                return value * inside(e)

            for bi, d in enumerate(group):

                def param(start, size):
                    return jnp.broadcast_to(
                        params_ref[start : start + size, block : block + 1], (size, width)
                    )

                scale_o = param(0, channels)
                shift_o = param(channels, channels)
                scale_i = param(2 * channels, mid)
                shift_i = param(2 * channels + mid, mid)

                def load(e):
                    return tile[e // rows, e % rows] if bi == 0 else stream_buf[e]

                for e in range(lo, hi):
                    value = jnp.maximum(load(e).astype(jnp.float32) * scale_o + shift_o, 0.0)
                    hidden_buf[e] = masked(value, e).astype(jnp.bfloat16)
                for e in range(lo + d, hi - d, 2):
                    both = jnp.concatenate(
                        [
                            jnp.concatenate([hidden_buf[e + i + (ky - 1) * d] for ky in range(3)], axis=0)
                            for i in range(2)
                        ],
                        axis=1,
                    )
                    y = jnp.dot(wn_ref[block], both, preferred_element_type=jnp.float32)
                    for i in range(2):
                        parts = [
                            y[kx * mid : (kx + 1) * mid, i * width : (i + 1) * width]
                            for kx in range(3)
                        ]
                        narrow = shifted_sum(parts, d, lane)
                        value = jnp.maximum(narrow * scale_i + shift_i, 0.0)
                        inner_buf[e + i] = masked(value, e + i).astype(jnp.bfloat16)
                lo, hi = lo + 2 * d, hi - 2 * d
                final = bi == len(group) - 1
                stream = [None] * rows
                for e in range(lo, hi, 2):
                    both = jnp.concatenate(
                        [
                            jnp.concatenate([inner_buf[e + i + (ky - 1) * d] for ky in range(3)], axis=0)
                            for i in range(2)
                        ],
                        axis=1,
                    )
                    y = jnp.dot(ww_ref[block], both, preferred_element_type=jnp.float32)
                    for i in range(2):
                        parts = [
                            y[kx * channels : (kx + 1) * channels, i * width : (i + 1) * width]
                            for kx in range(3)
                        ]
                        widened = shifted_sum(parts, d, lane)
                        value = (load(e + i).astype(jnp.float32) + widened).astype(jnp.bfloat16)
                        if final:
                            stream[e + i - lo] = value
                        else:
                            stream_buf[e + i] = value
                block += 1

    for r in range(rows):
        out_ref[r] = stream[r]

    for rd in range(rounds):

        def finish(k, carry):
            target = lax.rem(me + k, count)
            mirror_copy(rd, target, me).wait_send()
            return carry

        lax.fori_loop(1, count, finish, 0)
        for gi in range(groups):
            phase = rd * groups + gi
            tile = tiles[phase]
            reach = tile.shape[0] // 2
            for k in [s * k for k in range(1, reach + 1) for s in (-1, 1)]:

                @pl.when((me + k >= 0) & (me + k < count))
                def _():
                    remote(
                        tile.at[reach],
                        tile.at[reach - k],
                        halo_send.at[phase, reach + k],
                        halo_recv.at[phase, reach - k],
                        me + k,
                    ).wait_send()


def fused_body(features_in, gain_outer, bias_outer, w_narrow, gain_inner, bias_inner, w_widen):
    channels, rows, width = features_in.shape
    blocks, mid = gain_inner.shape
    count = lax.axis_size("row")
    rounds = blocks // sum(len(g) for g in GROUPS)
    halves = rows * channels // LANES
    pack, unpack = spread_constants(rows, channels, width)
    params = jnp.concatenate([gain_outer, bias_outer, gain_inner, bias_inner], axis=1).T
    wn = w_narrow.reshape(blocks, mid, 3, 3, channels).transpose(0, 3, 1, 2, 4)
    ww = w_widen.reshape(blocks, channels, 3, 3, mid).transpose(0, 3, 1, 2, 4)
    reaches = [-(-2 * sum(g) // rows) for g in GROUPS]
    tall = (2 * max(reaches) + 1) * rows
    phases = rounds * len(GROUPS)
    dma = pltpu.SemaphoreType.DMA
    out = pl.pallas_call(
        functools.partial(network_kernel, count, rounds),
        out_shape=jax.ShapeDtypeStruct((rows, channels, width), jnp.bfloat16),
        in_specs=[pl.BlockSpec(memory_space=pltpu.VMEM)] * 6,
        out_specs=pl.BlockSpec(memory_space=pltpu.VMEM),
        scratch_shapes=[
            pltpu.VMEM((2 * r + 1, rows, channels, width), jnp.bfloat16)
            for _ in range(rounds)
            for r in reaches
        ]
        + [
            pltpu.VMEM((rounds, count, rows * halves, LANES), jnp.bfloat16),
            pltpu.VMEM((rounds, count, rows * halves, LANES), jnp.bfloat16),
            pltpu.VMEM((tall, channels, width), jnp.bfloat16),
            pltpu.VMEM((tall, channels, width), jnp.bfloat16),
            pltpu.VMEM((tall, mid, width), jnp.bfloat16),
            dma((rounds, count)),
            dma((rounds, count)),
            dma((phases, 2 * max(reaches) + 1)),
            dma((phases, 2 * max(reaches) + 1)),
        ],
        compiler_params=pltpu.CompilerParams(
            collective_id=0, has_side_effects=True, vmem_limit_bytes=32 * 1024 * 1024
        ),
    )(
        features_in.transpose(1, 0, 2),
        params,
        wn.reshape(blocks, 3 * mid, 3 * channels),
        ww.reshape(blocks, 3 * channels, 3 * mid),
        pack,
        unpack,
    )
    return out.transpose(1, 0, 2)


def padded_2(block, sides, width):
    for axis, dim in sides:
        count = lax.axis_size(axis)
        forward = [(i, i + 1) for i in range(count - 1)]
        backward = [(target, source) for source, target in forward]
        low = lax.ppermute(
            lax.slice_in_dim(block, block.shape[dim] - width, None, axis=dim), axis, forward
        )
        high = lax.ppermute(lax.slice_in_dim(block, 0, width, axis=dim), axis, backward)
        block = jnp.concatenate([low, block, high], axis=dim)
    return block


def dilated_taps(padded, weight, dilation, rows, cols):
    channels = padded.shape[0]
    total = None
    for vertical in range(3):
        for lateral in range(3):
            tap_index = vertical * 3 + lateral
            window = padded[
                :,
                vertical * dilation : vertical * dilation + rows,
                lateral * dilation : lateral * dilation + cols,
            ]
            weight_tap = weight[:, tap_index * channels : (tap_index + 1) * channels]
            term = jnp.einsum("oc,crw->orw", weight_tap, window, preferred_element_type=jnp.float32)
            total = term if total is None else total + term
    return total


def mirrored(stream):
    channels = stream.shape[0]
    rows = stream.shape[1]
    width = stream.shape[2]
    row_count = lax.axis_size("row")
    core_count = lax.axis_size("col")
    squares = stream.reshape(channels, rows, row_count, core_count, rows)
    outgoing = squares.transpose(3, 2, 4, 1, 0).reshape(
        core_count, row_count, rows * rows * channels
    )
    received = lax.all_to_all(
        lax.all_to_all(outgoing, "row", split_axis=1, concat_axis=1, tiled=True),
        "col",
        split_axis=0,
        concat_axis=0,
        tiled=True,
    )
    partner = (
        received.reshape(core_count, row_count, rows, rows, channels)
        .transpose(4, 2, 1, 0, 3)
        .reshape(channels, rows, width)
    )
    return ((stream.astype(jnp.float32) + partner.astype(jnp.float32)) * 0.5).astype(jnp.bfloat16)


def averaged_tiles(stream):
    strips = lax.all_to_all(stream, "col", split_axis=1, concat_axis=2, tiled=True)
    merged = mirrored(strips)
    return lax.all_to_all(merged, "col", split_axis=2, concat_axis=1, tiled=True)


def inside_mask(row_start, col_start, offset, row_count, col_count, side):
    global_rows = row_start - offset + lax.iota(jnp.int32, row_count)
    global_cols = col_start - offset + lax.iota(jnp.int32, col_count)
    rows_ok = (global_rows >= 0) & (global_rows < side)
    cols_ok = (global_cols >= 0) & (global_cols < side)
    return (rows_ok[:, None] & cols_ok[None, :])[None]


def body(features_in, gain_outer, bias_outer, w_narrow, gain_inner, bias_inner, w_widen):
    stream = features_in
    rows = stream.shape[1]
    cols = stream.shape[2]
    side = rows * lax.axis_size("row")
    rounds = gain_outer.shape[0] // 4
    row_start = lax.axis_index("row") * rows
    col_start = lax.axis_index("col") * cols
    for repeat in range(rounds):
        stream = averaged_tiles(stream)
        for within in range(4):
            block = repeat * 4 + within
            dilation = 1 + within // 2
            outer_scale = gain_outer[block][:, None, None]
            outer_shift = bias_outer[block][:, None, None]
            inner_scale = gain_inner[block][:, None, None]
            inner_shift = bias_inner[block][:, None, None]
            deep = padded_2(stream, (("row", 1), ("col", 2)), 2 * dilation)
            hidden = jax.nn.relu(deep.astype(jnp.float32) * outer_scale + outer_shift)
            hidden = jnp.where(
                inside_mask(
                    row_start,
                    col_start,
                    2 * dilation,
                    rows + 4 * dilation,
                    cols + 4 * dilation,
                    side,
                ),
                hidden,
                0.0,
            ).astype(jnp.bfloat16)
            narrow = dilated_taps(
                hidden, w_narrow[block], dilation, rows + 2 * dilation, cols + 2 * dilation
            )
            inner = jax.nn.relu(narrow * inner_scale + inner_shift)
            inner = jnp.where(
                inside_mask(
                    row_start, col_start, dilation, rows + 2 * dilation, cols + 2 * dilation, side
                ),
                inner,
                0.0,
            ).astype(jnp.bfloat16)
            widened = dilated_taps(inner, w_widen[block], dilation, rows, cols)
            stream = (stream.astype(jnp.float32) + widened).astype(jnp.bfloat16)
    return stream


def dispatch(mesh, *args):
    channels, rows, width = args[0].shape
    whole_rows = mesh.shape["col"] == 1 and width == rows * mesh.shape["row"]
    packs = LANES % channels == 0 and rows * channels % LANES == 0 and width % LANES == 0
    even = rows % 2 == 0 and rows * rows * channels % (8 * LANES) == 0
    if whole_rows and packs and even:
        return fused_body(*args)
    return body(*args)


def solution(mesh):
    in_specs = (P(None, ("groups", "row"), "col"), P(), P(), P(), P(), P(), P())
    out_specs = P(None, ("groups", "row"), "col")
    return jax.shard_map(
        functools.partial(dispatch, mesh),
        mesh=mesh,
        in_specs=in_specs,
        out_specs=out_specs,
        check_vma=False,
    )
```

```python
import functools

import numpy as np
import jax
import jax.numpy as jnp
from jax import lax
from jax.experimental import pallas as pl
from jax.experimental.pallas import tpu as pltpu
from jax.sharding import PartitionSpec as P

GROUPS = ((1, 1), (2,), (2,))
LANES = 128


def remote(src, dst, send_sem, recv_sem, target):
    return pltpu.make_async_remote_copy(
        src_ref=src,
        dst_ref=dst,
        send_sem=send_sem,
        recv_sem=recv_sem,
        device_id={"row": target},
        device_id_type=pl.DeviceIdType.MESH,
    )


def spread_constants(rows, channels, width):
    count = width // rows
    halves = rows * channels // LANES
    pieces = rows * halves
    subs = LANES // channels
    p = np.arange(width * halves)
    pack = np.zeros((width * halves, halves * width), np.float32)
    pack[p, (p % halves) * width + p // halves] = 1
    o = np.arange(rows * width)
    xx, x = o // width, o % width
    j, r = x // rows, x % rows
    q = (r % subs) * (count * pieces) + j * pieces + xx * halves + r // subs
    unpack = np.zeros((subs * count * pieces, rows * width), np.float32)
    unpack[q, o] = 1
    return jnp.asarray(pack, jnp.bfloat16), jnp.asarray(unpack, jnp.bfloat16)


def shifted_sum(parts, dilation, lane):
    width = lane.shape[-1]
    low = jnp.where(lane < dilation, 0.0, pltpu.roll(parts[0], dilation, 1))
    high = jnp.where(lane >= width - dilation, 0.0, pltpu.roll(parts[2], width - dilation, 1))
    return parts[1] + low + high


def shifts(value, dilation, lane):
    width = lane.shape[-1]
    low = jnp.where(lane < dilation, 0.0, pltpu.roll(value, dilation, 1))
    high = jnp.where(lane >= width - dilation, 0.0, pltpu.roll(value, width - dilation, 1))
    return low, value, high


def network_kernel(
    count, rounds, x_ref, params_ref, raw_ref, ww_ref, pack_ref, unpack_ref, out_ref, *scratch
):
    rows, channels, width = x_ref.shape
    blocks, mid = raw_ref.shape[:2]
    side = rows * count
    halves = rows * channels // LANES
    subs = LANES // channels
    pieces = rows * halves
    groups = len(GROUPS)
    tiles = scratch[: rounds * groups]
    sent, got, stream_buf, hidden_buf, inner_buf, wn_ref = scratch[rounds * groups :][:6]
    mirror_send, mirror_recv, halo_send, halo_recv = scratch[rounds * groups + 6 :]
    me = lax.axis_index("row")

    def wrapped(k):
        t = me + k
        return jnp.where(t >= count, t - count, t)

    barrier = pltpu.get_barrier_semaphore()

    def greet(k, carry):
        pl.semaphore_signal(
            barrier,
            inc=1,
            device_id={"row": wrapped(k)},
            device_id_type=pl.DeviceIdType.MESH,
        )
        return carry

    lax.fori_loop(1, count, greet, 0)
    for phase in range(rounds * groups):
        tile = tiles[phase]
        reach = tile.shape[0] // 2
        for k in range(1, reach + 1):
            for sign in (-1, 1):
                slot = reach + sign * k
                other = me + sign * k

                @pl.when((other < 0) | (other >= count))
                def _():
                    tile[slot] = jnp.zeros(tile.shape[1:], tile.dtype)

    def pack(rd, stream):
        flat = [s for s in stream]
        per = LANES // channels
        cat = jnp.concatenate(
            [jnp.concatenate(flat[h * per : (h + 1) * per], axis=0) for h in range(halves)], axis=1
        )
        packed = lax.dot_general(
            pack_ref[...], cat, (((1,), (1,)), ((), ())), preferred_element_type=jnp.float32
        )
        sent[rd] = packed.reshape(count, pieces, LANES).astype(jnp.bfloat16)

    def mirror_copy(rd, target, source):
        return remote(
            sent.at[rd, target],
            got.at[rd, source],
            mirror_send.at[rd, target],
            mirror_recv.at[rd, source],
            target,
        )

    lane = lax.broadcasted_iota(jnp.int32, (1, width), 1)
    stream = [x_ref[r] for r in range(rows)]
    pack(0, stream)
    pl.semaphore_wait(barrier, count - 1)

    for rd in range(rounds):
        if rd:
            pack(rd, stream)

        def send(k, carry):
            mirror_copy(rd, wrapped(k), me).start()
            return carry

        def receive(k, carry):
            source = wrapped(k)
            mirror_copy(rd, source, source).wait_recv()
            return carry

        lax.fori_loop(1, count, send, 0)
        got[rd, me] = sent[rd, me]
        if rd == 0:
            def reorder(b, carry):
                raw = raw_ref[b]
                for kx in range(3):
                    taps = [(3 * ky + kx) * channels for ky in range(3)]
                    wn_ref[b, kx * mid : (kx + 1) * mid] = jnp.concatenate(
                        [raw[:, t : t + channels] for t in taps], axis=1
                    )
                return carry

            lax.fori_loop(0, blocks, reorder, 0)
        lax.fori_loop(1, count, receive, 0)

        arrived = got[rd].astype(jnp.float32).reshape(count * pieces, LANES).T
        arrived = jnp.concatenate(
            [arrived[u * channels : (u + 1) * channels] for u in range(subs)], axis=1
        ).astype(jnp.bfloat16)
        partner = jnp.dot(arrived, unpack_ref[...], preferred_element_type=jnp.float32)
        stream = [
            (
                (stream[r].astype(jnp.float32) + partner[:, r * width : (r + 1) * width]) * 0.5
            ).astype(jnp.bfloat16)
            for r in range(rows)
        ]

        block = rd * sum(len(g) for g in GROUPS)
        for gi, group in enumerate(GROUPS):
            phase = rd * groups + gi
            tile = tiles[phase]
            reach = tile.shape[0] // 2
            for r in range(rows):
                tile[reach, r] = stream[r]

            def halo_copy(k, slot_there, target):
                return remote(
                    tile.at[reach],
                    tile.at[slot_there],
                    halo_send.at[phase, reach + k],
                    halo_recv.at[phase, slot_there],
                    target,
                )

            offsets = [s * k for k in range(1, reach + 1) for s in (-1, 1)]
            for k in offsets:

                @pl.when((me + k >= 0) & (me + k < count))
                def _():
                    halo_copy(k, reach - k, me + k).start()

            halo = 2 * sum(group)
            lo = reach * rows - halo
            hi = (reach + 1) * rows + halo
            first_row = (me - reach) * rows

            def inside(e):
                g = first_row + e
                return jnp.where((g >= 0) & (g < side), 1.0, 0.0).astype(jnp.float32)

            def masked(value, e):
                if reach * rows <= e < (reach + 1) * rows:
                    return value
                return value * inside(e)

            for bi, d in enumerate(group):

                def param(start, size):
                    return jnp.broadcast_to(
                        params_ref[start : start + size, block : block + 1], (size, width)
                    )

                scale_o = param(0, channels)
                shift_o = param(channels, channels)
                scale_i = param(2 * channels, mid)
                shift_i = param(2 * channels + mid, mid)

                def load(e):
                    return tile[e // rows, e % rows] if bi == 0 else stream_buf[e]

                own = range(reach * rows, (reach + 1) * rows)
                outer = [e for e in range(lo, hi) if e not in own]
                for part in (own, outer):
                    if part is outer and bi == 0:
                        for k in offsets:

                            @pl.when((me + k >= 0) & (me + k < count))
                            def _():
                                halo_copy(k, reach + k, me + k).wait_recv()

                    for e in part:
                        value = jnp.maximum(load(e).astype(jnp.float32) * scale_o + shift_o, 0.0)
                        hidden_buf[e] = masked(value, e).astype(jnp.bfloat16)
                for e in range(lo + d, hi - d, 2):
                    both = jnp.concatenate(
                        [
                            jnp.concatenate([hidden_buf[e + i + (ky - 1) * d] for ky in range(3)], axis=0)
                            for i in range(2)
                        ],
                        axis=1,
                    )
                    y = jnp.dot(wn_ref[block], both, preferred_element_type=jnp.float32)
                    for i in range(2):
                        parts = [
                            y[kx * mid : (kx + 1) * mid, i * width : (i + 1) * width]
                            for kx in range(3)
                        ]
                        narrow = shifted_sum(parts, d, lane)
                        value = jnp.maximum(narrow * scale_i + shift_i, 0.0)
                        value = masked(value, e + i)
                        for kx, part in enumerate(shifts(value, d, lane)):
                            inner_buf[e + i, kx * mid : (kx + 1) * mid] = part.astype(jnp.bfloat16)
                lo, hi = lo + 2 * d, hi - 2 * d
                final = bi == len(group) - 1
                stream = [None] * rows
                for e in range(lo, hi, 2):
                    both = jnp.concatenate(
                        [
                            jnp.concatenate([inner_buf[e + i + (ky - 1) * d] for ky in range(3)], axis=0)
                            for i in range(2)
                        ],
                        axis=1,
                    )
                    y = jnp.dot(ww_ref[block], both, preferred_element_type=jnp.float32)
                    for i in range(2):
                        widened = y[:, i * width : (i + 1) * width]
                        value = (load(e + i).astype(jnp.float32) + widened).astype(jnp.bfloat16)
                        if final:
                            stream[e + i - lo] = value
                        else:
                            stream_buf[e + i] = value
                block += 1

    for r in range(rows):
        out_ref[r] = stream[r]

    for rd in range(rounds):

        def finish(k, carry):
            target = wrapped(k)
            mirror_copy(rd, target, me).wait_send()
            return carry

        lax.fori_loop(1, count, finish, 0)
        for gi in range(groups):
            phase = rd * groups + gi
            tile = tiles[phase]
            reach = tile.shape[0] // 2
            for k in [s * k for k in range(1, reach + 1) for s in (-1, 1)]:

                @pl.when((me + k >= 0) & (me + k < count))
                def _():
                    remote(
                        tile.at[reach],
                        tile.at[reach - k],
                        halo_send.at[phase, reach + k],
                        halo_recv.at[phase, reach - k],
                        me + k,
                    ).wait_send()


def fused_body(features_in, gain_outer, bias_outer, w_narrow, gain_inner, bias_inner, w_widen):
    channels, rows, width = features_in.shape
    blocks, mid = gain_inner.shape
    count = lax.axis_size("row")
    rounds = blocks // sum(len(g) for g in GROUPS)
    halves = rows * channels // LANES
    pack, unpack = spread_constants(rows, channels, width)
    params = jnp.concatenate([gain_outer, bias_outer, gain_inner, bias_inner], axis=1).T
    reaches = [-(-2 * sum(g) // rows) for g in GROUPS]
    tall = (2 * max(reaches) + 1) * rows
    phases = rounds * len(GROUPS)
    dma = pltpu.SemaphoreType.DMA
    out = pl.pallas_call(
        functools.partial(network_kernel, count, rounds),
        out_shape=jax.ShapeDtypeStruct((rows, channels, width), jnp.bfloat16),
        in_specs=[pl.BlockSpec(memory_space=pltpu.VMEM)] * 6,
        out_specs=pl.BlockSpec(memory_space=pltpu.VMEM),
        scratch_shapes=[
            pltpu.VMEM((2 * r + 1, rows, channels, width), jnp.bfloat16)
            for _ in range(rounds)
            for r in reaches
        ]
        + [
            pltpu.VMEM((rounds, count, rows * halves, LANES), jnp.bfloat16),
            pltpu.VMEM((rounds, count, rows * halves, LANES), jnp.bfloat16),
            pltpu.VMEM((tall, channels, width), jnp.bfloat16),
            pltpu.VMEM((tall, channels, width), jnp.bfloat16),
            pltpu.VMEM((tall, 3 * mid, width), jnp.bfloat16),
            pltpu.VMEM((blocks, 3 * mid, 3 * channels), jnp.bfloat16),
            dma((rounds, count)),
            dma((rounds, count)),
            dma((phases, 2 * max(reaches) + 1)),
            dma((phases, 2 * max(reaches) + 1)),
        ],
        compiler_params=pltpu.CompilerParams(
            collective_id=0, has_side_effects=True, vmem_limit_bytes=32 * 1024 * 1024
        ),
    )(
        features_in.transpose(1, 0, 2),
        params,
        w_narrow,
        w_widen,
        pack,
        unpack,
    )
    return out.transpose(1, 0, 2)


def padded_2(block, sides, width):
    for axis, dim in sides:
        count = lax.axis_size(axis)
        forward = [(i, i + 1) for i in range(count - 1)]
        backward = [(target, source) for source, target in forward]
        low = lax.ppermute(
            lax.slice_in_dim(block, block.shape[dim] - width, None, axis=dim), axis, forward
        )
        high = lax.ppermute(lax.slice_in_dim(block, 0, width, axis=dim), axis, backward)
        block = jnp.concatenate([low, block, high], axis=dim)
    return block


def dilated_taps(padded, weight, dilation, rows, cols):
    channels = padded.shape[0]
    total = None
    for vertical in range(3):
        for lateral in range(3):
            tap_index = vertical * 3 + lateral
            window = padded[
                :,
                vertical * dilation : vertical * dilation + rows,
                lateral * dilation : lateral * dilation + cols,
            ]
            weight_tap = weight[:, tap_index * channels : (tap_index + 1) * channels]
            term = jnp.einsum("oc,crw->orw", weight_tap, window, preferred_element_type=jnp.float32)
            total = term if total is None else total + term
    return total


def mirrored(stream):
    channels = stream.shape[0]
    rows = stream.shape[1]
    width = stream.shape[2]
    row_count = lax.axis_size("row")
    core_count = lax.axis_size("col")
    squares = stream.reshape(channels, rows, row_count, core_count, rows)
    outgoing = squares.transpose(3, 2, 4, 1, 0).reshape(
        core_count, row_count, rows * rows * channels
    )
    received = lax.all_to_all(
        lax.all_to_all(outgoing, "row", split_axis=1, concat_axis=1, tiled=True),
        "col",
        split_axis=0,
        concat_axis=0,
        tiled=True,
    )
    partner = (
        received.reshape(core_count, row_count, rows, rows, channels)
        .transpose(4, 2, 1, 0, 3)
        .reshape(channels, rows, width)
    )
    return ((stream.astype(jnp.float32) + partner.astype(jnp.float32)) * 0.5).astype(jnp.bfloat16)


def averaged_tiles(stream):
    strips = lax.all_to_all(stream, "col", split_axis=1, concat_axis=2, tiled=True)
    merged = mirrored(strips)
    return lax.all_to_all(merged, "col", split_axis=2, concat_axis=1, tiled=True)


def inside_mask(row_start, col_start, offset, row_count, col_count, side):
    global_rows = row_start - offset + lax.iota(jnp.int32, row_count)
    global_cols = col_start - offset + lax.iota(jnp.int32, col_count)
    rows_ok = (global_rows >= 0) & (global_rows < side)
    cols_ok = (global_cols >= 0) & (global_cols < side)
    return (rows_ok[:, None] & cols_ok[None, :])[None]


def body(features_in, gain_outer, bias_outer, w_narrow, gain_inner, bias_inner, w_widen):
    stream = features_in
    rows = stream.shape[1]
    cols = stream.shape[2]
    side = rows * lax.axis_size("row")
    rounds = gain_outer.shape[0] // 4
    row_start = lax.axis_index("row") * rows
    col_start = lax.axis_index("col") * cols
    for repeat in range(rounds):
        stream = averaged_tiles(stream)
        for within in range(4):
            block = repeat * 4 + within
            dilation = 1 + within // 2
            outer_scale = gain_outer[block][:, None, None]
            outer_shift = bias_outer[block][:, None, None]
            inner_scale = gain_inner[block][:, None, None]
            inner_shift = bias_inner[block][:, None, None]
            deep = padded_2(stream, (("row", 1), ("col", 2)), 2 * dilation)
            hidden = jax.nn.relu(deep.astype(jnp.float32) * outer_scale + outer_shift)
            hidden = jnp.where(
                inside_mask(
                    row_start,
                    col_start,
                    2 * dilation,
                    rows + 4 * dilation,
                    cols + 4 * dilation,
                    side,
                ),
                hidden,
                0.0,
            ).astype(jnp.bfloat16)
            narrow = dilated_taps(
                hidden, w_narrow[block], dilation, rows + 2 * dilation, cols + 2 * dilation
            )
            inner = jax.nn.relu(narrow * inner_scale + inner_shift)
            inner = jnp.where(
                inside_mask(
                    row_start, col_start, dilation, rows + 2 * dilation, cols + 2 * dilation, side
                ),
                inner,
                0.0,
            ).astype(jnp.bfloat16)
            widened = dilated_taps(inner, w_widen[block], dilation, rows, cols)
            stream = (stream.astype(jnp.float32) + widened).astype(jnp.bfloat16)
    return stream


def dispatch(mesh, *args):
    channels, rows, width = args[0].shape
    whole_rows = mesh.shape["col"] == 1 and width == rows * mesh.shape["row"]
    packs = LANES % channels == 0 and rows * channels % LANES == 0 and width % LANES == 0
    even = rows % 2 == 0 and rows * rows * channels % (8 * LANES) == 0
    if whole_rows and packs and even:
        return fused_body(*args)
    return body(*args)


def solution(mesh):
    in_specs = (P(None, ("groups", "row"), "col"), P(), P(), P(), P(), P(), P())
    out_specs = P(None, ("groups", "row"), "col")
    return jax.shard_map(
        functools.partial(dispatch, mesh),
        mesh=mesh,
        in_specs=in_specs,
        out_specs=out_specs,
        check_vma=False,
    )
```

```python
import functools

import numpy as np
import jax
import jax.numpy as jnp
from jax import lax
from jax.experimental import pallas as pl
from jax.experimental.pallas import tpu as pltpu
from jax.sharding import PartitionSpec as P

GROUPS = ((1, 1), (2,), (2,))
LANES = 128


def remote(src, dst, send_sem, recv_sem, target):
    return pltpu.make_async_remote_copy(
        src_ref=src,
        dst_ref=dst,
        send_sem=send_sem,
        recv_sem=recv_sem,
        device_id={"row": target},
        device_id_type=pl.DeviceIdType.MESH,
    )


def spread_constants(rows, channels, width):
    count = width // rows
    halves = rows * channels // LANES
    pieces = rows * halves
    subs = LANES // channels
    p = np.arange(width * halves)
    pack = np.zeros((width * halves, halves * width), np.float32)
    pack[p, (p % halves) * width + p // halves] = 1
    o = np.arange(rows * width)
    xx, x = o // width, o % width
    j, r = x // rows, x % rows
    q = (r % subs) * (count * pieces) + j * pieces + xx * halves + r // subs
    unpack = np.zeros((subs * count * pieces, rows * width), np.float32)
    unpack[q, o] = 1
    return jnp.asarray(pack), jnp.asarray(unpack)


def shifted_sum(parts, dilation, lane):
    width = lane.shape[-1]
    low = jnp.where(lane < dilation, 0.0, pltpu.roll(parts[0], dilation, 1))
    high = jnp.where(lane >= width - dilation, 0.0, pltpu.roll(parts[2], width - dilation, 1))
    return parts[1] + low + high


def shifts(value, dilation, lane):
    width = lane.shape[-1]
    low = jnp.where(lane < dilation, 0.0, pltpu.roll(value, dilation, 1))
    high = jnp.where(lane >= width - dilation, 0.0, pltpu.roll(value, width - dilation, 1))
    return low, value, high


def network_kernel(
    count, rounds, x_ref, *refs
):
    rows, channels, width = x_ref.shape
    hbm, out_ref, scratch = refs[:8], refs[8], refs[9:]
    held, held_sem, params_ref, scratch = scratch[:8], scratch[8], scratch[9], scratch[10:]
    pack_ref, unpack_ref, raw_ref, ww_ref = held[:4]
    blocks, mid = raw_ref.shape[:2]
    fetches = [
        pltpu.make_async_copy(source, target, held_sem.at[i])
        for i, (source, target) in enumerate(zip(hbm, held))
    ]
    for fetch in fetches:
        fetch.start()
    side = rows * count
    halves = rows * channels // LANES
    subs = LANES // channels
    pieces = rows * halves
    groups = len(GROUPS)
    tiles = scratch[: rounds * groups]
    sent, got, stream_buf, hidden_buf, inner_buf, wn_ref = scratch[rounds * groups :][:6]
    mirror_send, mirror_recv, halo_send, halo_recv = scratch[rounds * groups + 6 :]
    me = lax.axis_index("row")

    def wrapped(k):
        t = me + k
        return jnp.where(t >= count, t - count, t)

    barrier = pltpu.get_barrier_semaphore()

    def greet(k, carry):
        pl.semaphore_signal(
            barrier,
            inc=1,
            device_id={"row": wrapped(k)},
            device_id_type=pl.DeviceIdType.MESH,
        )
        return carry

    lax.fori_loop(1, count, greet, 0)
    for phase in range(rounds * groups):
        tile = tiles[phase]
        reach = tile.shape[0] // 2
        for k in range(1, reach + 1):
            for sign in (-1, 1):
                slot = reach + sign * k
                other = me + sign * k

                @pl.when((other < 0) | (other >= count))
                def _():
                    tile[slot] = jnp.zeros(tile.shape[1:], tile.dtype)

    def pack(rd, stream):
        flat = [s for s in stream]
        per = LANES // channels
        cat = jnp.concatenate(
            [jnp.concatenate(flat[h * per : (h + 1) * per], axis=0) for h in range(halves)], axis=1
        )
        packed = lax.dot_general(
            pack_ref[...].astype(jnp.bfloat16), cat, (((1,), (1,)), ((), ())), preferred_element_type=jnp.float32
        )
        sent[rd] = packed.reshape(count, pieces, LANES).astype(jnp.bfloat16)

    def mirror_copy(rd, target, source):
        return remote(
            sent.at[rd, target],
            got.at[rd, source],
            mirror_send.at[rd],
            mirror_recv.at[rd],
            target,
        )

    def mirror_all(rd):
        rest = pl.ds(0, count - 1)
        return remote(
            sent.at[rd, rest],
            got.at[rd, rest],
            mirror_send.at[rd],
            mirror_recv.at[rd],
            wrapped(1),
        )

    lane = lax.broadcasted_iota(jnp.int32, (1, width), 1)
    stream = [x_ref[r] for r in range(rows)]
    fetches[0].wait()
    pack(0, stream)
    pl.semaphore_wait(barrier, count - 1)

    for rd in range(rounds):
        if rd:
            pack(rd, stream)

        def send(k, carry):
            mirror_copy(rd, wrapped(k), me).start()
            return carry

        lax.fori_loop(1, count, send, 0)
        got[rd, me] = sent[rd, me]
        if rd == 0:
            for fetch in fetches[1:]:
                fetch.wait()
            outer = jnp.concatenate([held[4][...], held[5][...]], axis=1)
            inner = jnp.concatenate([held[6][...], held[7][...]], axis=1)
            params_ref[: 2 * channels] = outer.T
            params_ref[2 * channels :] = inner.T

            def reorder(b, carry):
                raw = raw_ref[b]
                for kx in range(3):
                    taps = [(3 * ky + kx) * channels for ky in range(3)]
                    wn_ref[b, kx * mid : (kx + 1) * mid] = jnp.concatenate(
                        [raw[:, t : t + channels] for t in taps], axis=1
                    )
                return carry

            lax.fori_loop(0, blocks, reorder, 0)
        mirror_all(rd).wait_recv()

        arrived = got[rd].astype(jnp.float32).reshape(count * pieces, LANES).T
        arrived = jnp.concatenate(
            [arrived[u * channels : (u + 1) * channels] for u in range(subs)], axis=1
        ).astype(jnp.bfloat16)
        partner = jnp.dot(
            arrived, unpack_ref[...].astype(jnp.bfloat16), preferred_element_type=jnp.float32
        )
        stream = [
            (
                (stream[r].astype(jnp.float32) + partner[:, r * width : (r + 1) * width]) * 0.5
            ).astype(jnp.bfloat16)
            for r in range(rows)
        ]

        block = rd * sum(len(g) for g in GROUPS)
        for gi, group in enumerate(GROUPS):
            phase = rd * groups + gi
            tile = tiles[phase]
            reach = tile.shape[0] // 2
            for r in range(rows):
                tile[reach, r] = stream[r]

            def halo_copy(k, slot_there, target):
                return remote(
                    tile.at[reach],
                    tile.at[slot_there],
                    halo_send.at[phase, reach + k],
                    halo_recv.at[phase, slot_there],
                    target,
                )

            offsets = [s * k for k in range(1, reach + 1) for s in (-1, 1)]
            for k in offsets:

                @pl.when((me + k >= 0) & (me + k < count))
                def _():
                    halo_copy(k, reach - k, me + k).start()

            halo = 2 * sum(group)
            lo = reach * rows - halo
            hi = (reach + 1) * rows + halo
            first_row = (me - reach) * rows

            def inside(e):
                g = first_row + e
                return jnp.where((g >= 0) & (g < side), 1.0, 0.0).astype(jnp.float32)

            def masked(value, e):
                if reach * rows <= e < (reach + 1) * rows:
                    return value
                return value * inside(e)

            for bi, d in enumerate(group):

                def param(start, size):
                    return jnp.broadcast_to(
                        params_ref[start : start + size, block : block + 1], (size, width)
                    )

                scale_o = param(0, channels)
                shift_o = param(channels, channels)
                scale_i = param(2 * channels, mid)
                shift_i = param(2 * channels + mid, mid)

                def load(e):
                    return tile[e // rows, e % rows] if bi == 0 else stream_buf[e]

                own = range(reach * rows, (reach + 1) * rows)
                outer = [e for e in range(lo, hi) if e not in own]
                for part in (own, outer):
                    if part is outer and bi == 0:
                        for k in offsets:

                            @pl.when((me + k >= 0) & (me + k < count))
                            def _():
                                halo_copy(k, reach + k, me + k).wait_recv()

                    for e in part:
                        value = jnp.maximum(load(e).astype(jnp.float32) * scale_o + shift_o, 0.0)
                        hidden_buf[e] = masked(value, e).astype(jnp.bfloat16)
                for e, some in [(lo + d, hi - lo - 2 * d)]:
                    both = jnp.concatenate(
                        [
                            jnp.concatenate([hidden_buf[e + i + (ky - 1) * d] for ky in range(3)], axis=0)
                            for i in range(some)
                        ],
                        axis=1,
                    )
                    y = jnp.dot(wn_ref[block], both, preferred_element_type=jnp.float32)
                    for i in range(some):
                        parts = [
                            y[kx * mid : (kx + 1) * mid, i * width : (i + 1) * width]
                            for kx in range(3)
                        ]
                        narrow = shifted_sum(parts, d, lane)
                        value = jnp.maximum(narrow * scale_i + shift_i, 0.0)
                        value = masked(value, e + i)
                        for kx, part in enumerate(shifts(value, d, lane)):
                            inner_buf[e + i, kx * mid : (kx + 1) * mid] = part.astype(jnp.bfloat16)
                lo, hi = lo + 2 * d, hi - 2 * d
                final = bi == len(group) - 1
                stream = [None] * rows
                for e, some in [(lo, hi - lo)]:
                    both = jnp.concatenate(
                        [
                            jnp.concatenate([inner_buf[e + i + (ky - 1) * d] for ky in range(3)], axis=0)
                            for i in range(some)
                        ],
                        axis=1,
                    )
                    y = jnp.dot(ww_ref[block], both, preferred_element_type=jnp.float32)
                    for i in range(some):
                        widened = y[:, i * width : (i + 1) * width]
                        value = (load(e + i).astype(jnp.float32) + widened).astype(jnp.bfloat16)
                        if final:
                            stream[e + i - lo] = value
                        else:
                            stream_buf[e + i] = value
                block += 1

    for r in range(rows):
        out_ref[r] = stream[r]

    for rd in range(rounds):
        mirror_all(rd).wait_send()
        for gi in range(groups):
            phase = rd * groups + gi
            tile = tiles[phase]
            reach = tile.shape[0] // 2
            for k in [s * k for k in range(1, reach + 1) for s in (-1, 1)]:

                @pl.when((me + k >= 0) & (me + k < count))
                def _():
                    remote(
                        tile.at[reach],
                        tile.at[reach - k],
                        halo_send.at[phase, reach + k],
                        halo_recv.at[phase, reach - k],
                        me + k,
                    ).wait_send()


def fused_body(features_in, gain_outer, bias_outer, w_narrow, gain_inner, bias_inner, w_widen):
    channels, rows, width = features_in.shape
    blocks, mid = gain_inner.shape
    count = lax.axis_size("row")
    rounds = blocks // sum(len(g) for g in GROUPS)
    halves = rows * channels // LANES
    pack, unpack = spread_constants(rows, channels, width)
    fetched = (pack, unpack, w_narrow, w_widen, gain_outer, bias_outer, gain_inner, bias_inner)
    reaches = [-(-2 * sum(g) // rows) for g in GROUPS]
    tall = (2 * max(reaches) + 1) * rows
    phases = rounds * len(GROUPS)
    dma = pltpu.SemaphoreType.DMA
    out = pl.pallas_call(
        functools.partial(network_kernel, count, rounds),
        out_shape=jax.ShapeDtypeStruct((rows, channels, width), jnp.bfloat16),
        in_specs=[pl.BlockSpec(memory_space=pltpu.VMEM)]
        + [pl.BlockSpec(memory_space=pltpu.HBM)] * len(fetched),
        out_specs=pl.BlockSpec(memory_space=pltpu.VMEM),
        scratch_shapes=[pltpu.VMEM(a.shape, a.dtype) for a in fetched]
        + [dma((len(fetched),)), pltpu.VMEM((2 * (channels + mid), blocks), jnp.float32)]
        + [
            pltpu.VMEM((2 * r + 1, rows, channels, width), jnp.bfloat16)
            for _ in range(rounds)
            for r in reaches
        ]
        + [
            pltpu.VMEM((rounds, count, rows * halves, LANES), jnp.bfloat16),
            pltpu.VMEM((rounds, count, rows * halves, LANES), jnp.bfloat16),
            pltpu.VMEM((tall, channels, width), jnp.bfloat16),
            pltpu.VMEM((tall, channels, width), jnp.bfloat16),
            pltpu.VMEM((tall, 3 * mid, width), jnp.bfloat16),
            pltpu.VMEM((blocks, 3 * mid, 3 * channels), jnp.bfloat16),
            dma((rounds,)),
            dma((rounds,)),
            dma((phases, 2 * max(reaches) + 1)),
            dma((phases, 2 * max(reaches) + 1)),
        ],
        compiler_params=pltpu.CompilerParams(
            collective_id=0, has_side_effects=True, vmem_limit_bytes=60 * 1024 * 1024
        ),
    )(
        features_in.transpose(1, 0, 2),
        *fetched,
    )
    return out.transpose(1, 0, 2)


def padded_2(block, sides, width):
    for axis, dim in sides:
        count = lax.axis_size(axis)
        forward = [(i, i + 1) for i in range(count - 1)]
        backward = [(target, source) for source, target in forward]
        low = lax.ppermute(
            lax.slice_in_dim(block, block.shape[dim] - width, None, axis=dim), axis, forward
        )
        high = lax.ppermute(lax.slice_in_dim(block, 0, width, axis=dim), axis, backward)
        block = jnp.concatenate([low, block, high], axis=dim)
    return block


def dilated_taps(padded, weight, dilation, rows, cols):
    channels = padded.shape[0]
    total = None
    for vertical in range(3):
        for lateral in range(3):
            tap_index = vertical * 3 + lateral
            window = padded[
                :,
                vertical * dilation : vertical * dilation + rows,
                lateral * dilation : lateral * dilation + cols,
            ]
            weight_tap = weight[:, tap_index * channels : (tap_index + 1) * channels]
            term = jnp.einsum("oc,crw->orw", weight_tap, window, preferred_element_type=jnp.float32)
            total = term if total is None else total + term
    return total


def mirrored(stream):
    channels = stream.shape[0]
    rows = stream.shape[1]
    width = stream.shape[2]
    row_count = lax.axis_size("row")
    core_count = lax.axis_size("col")
    squares = stream.reshape(channels, rows, row_count, core_count, rows)
    outgoing = squares.transpose(3, 2, 4, 1, 0).reshape(
        core_count, row_count, rows * rows * channels
    )
    received = lax.all_to_all(
        lax.all_to_all(outgoing, "row", split_axis=1, concat_axis=1, tiled=True),
        "col",
        split_axis=0,
        concat_axis=0,
        tiled=True,
    )
    partner = (
        received.reshape(core_count, row_count, rows, rows, channels)
        .transpose(4, 2, 1, 0, 3)
        .reshape(channels, rows, width)
    )
    return ((stream.astype(jnp.float32) + partner.astype(jnp.float32)) * 0.5).astype(jnp.bfloat16)


def averaged_tiles(stream):
    strips = lax.all_to_all(stream, "col", split_axis=1, concat_axis=2, tiled=True)
    merged = mirrored(strips)
    return lax.all_to_all(merged, "col", split_axis=2, concat_axis=1, tiled=True)


def inside_mask(row_start, col_start, offset, row_count, col_count, side):
    global_rows = row_start - offset + lax.iota(jnp.int32, row_count)
    global_cols = col_start - offset + lax.iota(jnp.int32, col_count)
    rows_ok = (global_rows >= 0) & (global_rows < side)
    cols_ok = (global_cols >= 0) & (global_cols < side)
    return (rows_ok[:, None] & cols_ok[None, :])[None]


def body(features_in, gain_outer, bias_outer, w_narrow, gain_inner, bias_inner, w_widen):
    stream = features_in
    rows = stream.shape[1]
    cols = stream.shape[2]
    side = rows * lax.axis_size("row")
    rounds = gain_outer.shape[0] // 4
    row_start = lax.axis_index("row") * rows
    col_start = lax.axis_index("col") * cols
    for repeat in range(rounds):
        stream = averaged_tiles(stream)
        for within in range(4):
            block = repeat * 4 + within
            dilation = 1 + within // 2
            outer_scale = gain_outer[block][:, None, None]
            outer_shift = bias_outer[block][:, None, None]
            inner_scale = gain_inner[block][:, None, None]
            inner_shift = bias_inner[block][:, None, None]
            deep = padded_2(stream, (("row", 1), ("col", 2)), 2 * dilation)
            hidden = jax.nn.relu(deep.astype(jnp.float32) * outer_scale + outer_shift)
            hidden = jnp.where(
                inside_mask(
                    row_start,
                    col_start,
                    2 * dilation,
                    rows + 4 * dilation,
                    cols + 4 * dilation,
                    side,
                ),
                hidden,
                0.0,
            ).astype(jnp.bfloat16)
            narrow = dilated_taps(
                hidden, w_narrow[block], dilation, rows + 2 * dilation, cols + 2 * dilation
            )
            inner = jax.nn.relu(narrow * inner_scale + inner_shift)
            inner = jnp.where(
                inside_mask(
                    row_start, col_start, dilation, rows + 2 * dilation, cols + 2 * dilation, side
                ),
                inner,
                0.0,
            ).astype(jnp.bfloat16)
            widened = dilated_taps(inner, w_widen[block], dilation, rows, cols)
            stream = (stream.astype(jnp.float32) + widened).astype(jnp.bfloat16)
    return stream


def dispatch(mesh, *args):
    channels, rows, width = args[0].shape
    whole_rows = mesh.shape["col"] == 1 and width == rows * mesh.shape["row"]
    packs = LANES % channels == 0 and rows * channels % LANES == 0 and width % LANES == 0
    even = rows % 2 == 0 and rows * rows * channels % (8 * LANES) == 0
    if whole_rows and packs and even:
        return fused_body(*args)
    return body(*args)


def solution(mesh):
    in_specs = (P(None, ("groups", "row"), "col"), P(), P(), P(), P(), P(), P())
    out_specs = P(None, ("groups", "row"), "col")
    return jax.shard_map(
        functools.partial(dispatch, mesh),
        mesh=mesh,
        in_specs=in_specs,
        out_specs=out_specs,
        check_vma=False,
    )
```

```python
import functools

import numpy as np
import jax
import jax.numpy as jnp
from jax import lax
from jax.experimental import pallas as pl
from jax.experimental.pallas import tpu as pltpu
from jax.sharding import PartitionSpec as P

GROUPS = ((1, 1), (2,), (2,))
LANES = 128


def remote(src, dst, send_sem, recv_sem, target):
    return pltpu.make_async_remote_copy(
        src_ref=src,
        dst_ref=dst,
        send_sem=send_sem,
        recv_sem=recv_sem,
        device_id={"row": target},
        device_id_type=pl.DeviceIdType.MESH,
    )


def spread_constants(rows, channels, width):
    count = width // rows
    halves = rows * channels // LANES
    pieces = rows * halves
    subs = LANES // channels
    p = np.arange(width * halves)
    pack = np.zeros((width * halves, halves * width), np.float32)
    pack[p, (p % halves) * width + p // halves] = 1
    o = np.arange(rows * width)
    xx, x = o // width, o % width
    j, r = x // rows, x % rows
    q = (r % subs) * (count * pieces) + j * pieces + xx * halves + r // subs
    unpack = np.zeros((subs * count * pieces, rows * width), np.float32)
    unpack[q, o] = 1
    return jnp.asarray(pack), jnp.asarray(unpack)


def shifted_sum(parts, dilation, lane):
    width = lane.shape[-1]
    low = jnp.where(lane < dilation, 0.0, pltpu.roll(parts[0], dilation, 1))
    high = jnp.where(lane >= width - dilation, 0.0, pltpu.roll(parts[2], width - dilation, 1))
    return parts[1] + low + high


def shifts(value, dilation, lane):
    width = lane.shape[-1]
    low = jnp.where(lane < dilation, 0.0, pltpu.roll(value, dilation, 1))
    high = jnp.where(lane >= width - dilation, 0.0, pltpu.roll(value, width - dilation, 1))
    return low, value, high


def network_kernel(
    count, rounds, x_ref, *refs
):
    channels, rows, width = x_ref.shape
    hbm, out_ref, scratch = refs[:8], refs[8], refs[9:]
    held, held_sem, params_ref, x_wide = scratch[:8], scratch[8], scratch[9], scratch[10]
    scratch = scratch[11:]
    pack_ref, unpack_ref, raw_ref, ww_ref = held[:4]
    blocks, mid = raw_ref.shape[:2]
    fetches = [
        pltpu.make_async_copy(source, target, held_sem.at[i])
        for i, (source, target) in enumerate(zip(hbm, held))
    ]
    for fetch in fetches:
        fetch.start()
    side = rows * count
    halves = rows * channels // LANES
    subs = LANES // channels
    pieces = rows * halves
    groups = len(GROUPS)
    tiles = scratch[: rounds * groups]
    sent, got, stream_buf, hidden_buf, inner_buf, wn_ref = scratch[rounds * groups :][:6]
    mirror_send, mirror_recv, halo_send, halo_recv = scratch[rounds * groups + 6 :]
    me = lax.axis_index("row")

    def wrapped(k):
        t = me + k
        return jnp.where(t >= count, t - count, t)

    barrier = pltpu.get_barrier_semaphore()

    far_first = sorted(range(1, count), key=lambda k: -min(k, count - k))

    def greet(k):
        pl.semaphore_signal(
            barrier,
            inc=1,
            device_id={"row": wrapped(k)},
            device_id_type=pl.DeviceIdType.MESH,
        )

    for k in far_first:
        greet(k)
    for phase in range(rounds * groups):
        tile = tiles[phase]
        reach = tile.shape[0] // 2
        for k in range(1, reach + 1):
            for sign in (-1, 1):
                slot = reach + sign * k
                other = me + sign * k

                @pl.when((other < 0) | (other >= count))
                def _():
                    tile[slot] = jnp.zeros(tile.shape[1:], tile.dtype)

    def pack(rd, stream):
        flat = [s for s in stream]
        per = LANES // channels
        cat = jnp.concatenate(
            [jnp.concatenate(flat[h * per : (h + 1) * per], axis=0) for h in range(halves)], axis=1
        )
        packed = lax.dot_general(
            pack_ref[...].astype(jnp.bfloat16), cat, (((1,), (1,)), ((), ())), preferred_element_type=jnp.float32
        )
        sent[rd] = packed.reshape(count, pieces, LANES).astype(jnp.bfloat16)

    def mirror_copy(rd, target, source):
        return remote(
            sent.at[rd, target],
            got.at[rd, source],
            mirror_send.at[rd],
            mirror_recv.at[rd],
            target,
        )

    def mirror_all(rd):
        rest = pl.ds(0, count - 1)
        return remote(
            sent.at[rd, rest],
            got.at[rd, rest],
            mirror_send.at[rd],
            mirror_recv.at[rd],
            wrapped(1),
        )

    lane = lax.broadcasted_iota(jnp.int32, (1, width), 1)
    x_wide[...] = x_ref[...].astype(jnp.float32)
    stream = [x_wide[:, r, :].astype(jnp.bfloat16) for r in range(rows)]
    fetches[0].wait()
    pack(0, stream)
    pl.semaphore_wait(barrier, count - 1)

    for rd in range(rounds):
        if rd:
            pack(rd, stream)

        for k in far_first:
            mirror_copy(rd, wrapped(k), me).start()
        got[rd, me] = sent[rd, me]
        if rd == 0:
            for fetch in fetches[1:]:
                fetch.wait()
            outer = jnp.concatenate([held[4][...], held[5][...]], axis=1)
            inner = jnp.concatenate([held[6][...], held[7][...]], axis=1)
            params_ref[: 2 * channels] = outer.T
            params_ref[2 * channels :] = inner.T

            def reorder(b, carry):
                raw = raw_ref[b]
                for kx in range(3):
                    taps = [(3 * ky + kx) * channels for ky in range(3)]
                    wn_ref[b, kx * mid : (kx + 1) * mid] = jnp.concatenate(
                        [raw[:, t : t + channels] for t in taps], axis=1
                    )
                return carry

            lax.fori_loop(0, blocks, reorder, 0)
        mirror_all(rd).wait_recv()

        arrived = got[rd].astype(jnp.float32).reshape(count * pieces, LANES).T
        arrived = jnp.concatenate(
            [arrived[u * channels : (u + 1) * channels] for u in range(subs)], axis=1
        ).astype(jnp.bfloat16)
        partner = jnp.dot(
            arrived, unpack_ref[...].astype(jnp.bfloat16), preferred_element_type=jnp.float32
        )
        stream = [
            (
                (stream[r].astype(jnp.float32) + partner[:, r * width : (r + 1) * width]) * 0.5
            ).astype(jnp.bfloat16)
            for r in range(rows)
        ]

        block = rd * sum(len(g) for g in GROUPS)
        for gi, group in enumerate(GROUPS):
            phase = rd * groups + gi
            tile = tiles[phase]
            reach = tile.shape[0] // 2
            for r in range(rows):
                tile[reach, r] = stream[r]

            def halo_copy(k, slot_there, target):
                return remote(
                    tile.at[reach],
                    tile.at[slot_there],
                    halo_send.at[phase, reach + k],
                    halo_recv.at[phase, slot_there],
                    target,
                )

            offsets = [s * k for k in range(1, reach + 1) for s in (-1, 1)]
            for k in offsets:

                @pl.when((me + k >= 0) & (me + k < count))
                def _():
                    halo_copy(k, reach - k, me + k).start()

            halo = 2 * sum(group)
            lo = reach * rows - halo
            hi = (reach + 1) * rows + halo
            first_row = (me - reach) * rows

            def inside(e):
                g = first_row + e
                return jnp.where((g >= 0) & (g < side), 1.0, 0.0).astype(jnp.float32)

            def masked(value, e):
                if reach * rows <= e < (reach + 1) * rows:
                    return value
                return value * inside(e)

            for bi, d in enumerate(group):

                def param(start, size):
                    return jnp.broadcast_to(
                        params_ref[start : start + size, block : block + 1], (size, width)
                    )

                scale_o = param(0, channels)
                shift_o = param(channels, channels)
                scale_i = param(2 * channels, mid)
                shift_i = param(2 * channels + mid, mid)

                def load(e):
                    return tile[e // rows, e % rows] if bi == 0 else stream_buf[e]

                own = range(reach * rows, (reach + 1) * rows)
                outer = [e for e in range(lo, hi) if e not in own]
                for part in (own, outer):
                    if part is outer and bi == 0:
                        for k in offsets:

                            @pl.when((me + k >= 0) & (me + k < count))
                            def _():
                                halo_copy(k, reach + k, me + k).wait_recv()

                    for e in part:
                        value = jnp.maximum(load(e).astype(jnp.float32) * scale_o + shift_o, 0.0)
                        hidden_buf[e] = masked(value, e).astype(jnp.bfloat16)
                for e, some in [(lo + d, hi - lo - 2 * d)]:
                    both = jnp.concatenate(
                        [
                            jnp.concatenate([hidden_buf[e + i + (ky - 1) * d] for ky in range(3)], axis=0)
                            for i in range(some)
                        ],
                        axis=1,
                    )
                    y = jnp.dot(wn_ref[block], both, preferred_element_type=jnp.float32)
                    for i in range(some):
                        parts = [
                            y[kx * mid : (kx + 1) * mid, i * width : (i + 1) * width]
                            for kx in range(3)
                        ]
                        narrow = shifted_sum(parts, d, lane)
                        value = jnp.maximum(narrow * scale_i + shift_i, 0.0)
                        value = masked(value, e + i)
                        for kx, part in enumerate(shifts(value, d, lane)):
                            inner_buf[e + i, kx * mid : (kx + 1) * mid] = part.astype(jnp.bfloat16)
                lo, hi = lo + 2 * d, hi - 2 * d
                final = bi == len(group) - 1
                stream = [None] * rows
                for e, some in [(lo, hi - lo)]:
                    both = jnp.concatenate(
                        [
                            jnp.concatenate([inner_buf[e + i + (ky - 1) * d] for ky in range(3)], axis=0)
                            for i in range(some)
                        ],
                        axis=1,
                    )
                    y = jnp.dot(ww_ref[block], both, preferred_element_type=jnp.float32)
                    for i in range(some):
                        widened = y[:, i * width : (i + 1) * width]
                        value = (load(e + i).astype(jnp.float32) + widened).astype(jnp.bfloat16)
                        if final:
                            stream[e + i - lo] = value
                        else:
                            stream_buf[e + i] = value
                block += 1

    for r in range(rows):
        out_ref[r] = stream[r]

    for rd in range(rounds):
        mirror_all(rd).wait_send()
        for gi in range(groups):
            phase = rd * groups + gi
            tile = tiles[phase]
            reach = tile.shape[0] // 2
            for k in [s * k for k in range(1, reach + 1) for s in (-1, 1)]:

                @pl.when((me + k >= 0) & (me + k < count))
                def _():
                    remote(
                        tile.at[reach],
                        tile.at[reach - k],
                        halo_send.at[phase, reach + k],
                        halo_recv.at[phase, reach - k],
                        me + k,
                    ).wait_send()


def fused_body(features_in, gain_outer, bias_outer, w_narrow, gain_inner, bias_inner, w_widen):
    channels, rows, width = features_in.shape
    blocks, mid = gain_inner.shape
    count = lax.axis_size("row")
    rounds = blocks // sum(len(g) for g in GROUPS)
    halves = rows * channels // LANES
    pack, unpack = spread_constants(rows, channels, width)
    fetched = (pack, unpack, w_narrow, w_widen, gain_outer, bias_outer, gain_inner, bias_inner)
    reaches = [-(-2 * sum(g) // rows) for g in GROUPS]
    tall = (2 * max(reaches) + 1) * rows
    phases = rounds * len(GROUPS)
    dma = pltpu.SemaphoreType.DMA
    out = pl.pallas_call(
        functools.partial(network_kernel, count, rounds),
        out_shape=jax.ShapeDtypeStruct((rows, channels, width), jnp.bfloat16),
        in_specs=[pl.BlockSpec(memory_space=pltpu.VMEM)]
        + [pl.BlockSpec(memory_space=pltpu.HBM)] * len(fetched),
        out_specs=pl.BlockSpec(memory_space=pltpu.VMEM),
        scratch_shapes=[pltpu.VMEM(a.shape, a.dtype) for a in fetched]
        + [dma((len(fetched),)), pltpu.VMEM((2 * (channels + mid), blocks), jnp.float32)]
        + [pltpu.VMEM(features_in.shape, jnp.float32)]
        + [
            pltpu.VMEM((2 * r + 1, rows, channels, width), jnp.bfloat16)
            for _ in range(rounds)
            for r in reaches
        ]
        + [
            pltpu.VMEM((rounds, count, rows * halves, LANES), jnp.bfloat16),
            pltpu.VMEM((rounds, count, rows * halves, LANES), jnp.bfloat16),
            pltpu.VMEM((tall, channels, width), jnp.bfloat16),
            pltpu.VMEM((tall, channels, width), jnp.bfloat16),
            pltpu.VMEM((tall, 3 * mid, width), jnp.bfloat16),
            pltpu.VMEM((blocks, 3 * mid, 3 * channels), jnp.bfloat16),
            dma((rounds,)),
            dma((rounds,)),
            dma((phases, 2 * max(reaches) + 1)),
            dma((phases, 2 * max(reaches) + 1)),
        ],
        compiler_params=pltpu.CompilerParams(
            collective_id=0, has_side_effects=True, vmem_limit_bytes=60 * 1024 * 1024
        ),
    )(
        features_in,
        *fetched,
    )
    return out.transpose(1, 0, 2)


def padded_2(block, sides, width):
    for axis, dim in sides:
        count = lax.axis_size(axis)
        forward = [(i, i + 1) for i in range(count - 1)]
        backward = [(target, source) for source, target in forward]
        low = lax.ppermute(
            lax.slice_in_dim(block, block.shape[dim] - width, None, axis=dim), axis, forward
        )
        high = lax.ppermute(lax.slice_in_dim(block, 0, width, axis=dim), axis, backward)
        block = jnp.concatenate([low, block, high], axis=dim)
    return block


def dilated_taps(padded, weight, dilation, rows, cols):
    channels = padded.shape[0]
    total = None
    for vertical in range(3):
        for lateral in range(3):
            tap_index = vertical * 3 + lateral
            window = padded[
                :,
                vertical * dilation : vertical * dilation + rows,
                lateral * dilation : lateral * dilation + cols,
            ]
            weight_tap = weight[:, tap_index * channels : (tap_index + 1) * channels]
            term = jnp.einsum("oc,crw->orw", weight_tap, window, preferred_element_type=jnp.float32)
            total = term if total is None else total + term
    return total


def mirrored(stream):
    channels = stream.shape[0]
    rows = stream.shape[1]
    width = stream.shape[2]
    row_count = lax.axis_size("row")
    core_count = lax.axis_size("col")
    squares = stream.reshape(channels, rows, row_count, core_count, rows)
    outgoing = squares.transpose(3, 2, 4, 1, 0).reshape(
        core_count, row_count, rows * rows * channels
    )
    received = lax.all_to_all(
        lax.all_to_all(outgoing, "row", split_axis=1, concat_axis=1, tiled=True),
        "col",
        split_axis=0,
        concat_axis=0,
        tiled=True,
    )
    partner = (
        received.reshape(core_count, row_count, rows, rows, channels)
        .transpose(4, 2, 1, 0, 3)
        .reshape(channels, rows, width)
    )
    return ((stream.astype(jnp.float32) + partner.astype(jnp.float32)) * 0.5).astype(jnp.bfloat16)


def averaged_tiles(stream):
    strips = lax.all_to_all(stream, "col", split_axis=1, concat_axis=2, tiled=True)
    merged = mirrored(strips)
    return lax.all_to_all(merged, "col", split_axis=2, concat_axis=1, tiled=True)


def inside_mask(row_start, col_start, offset, row_count, col_count, side):
    global_rows = row_start - offset + lax.iota(jnp.int32, row_count)
    global_cols = col_start - offset + lax.iota(jnp.int32, col_count)
    rows_ok = (global_rows >= 0) & (global_rows < side)
    cols_ok = (global_cols >= 0) & (global_cols < side)
    return (rows_ok[:, None] & cols_ok[None, :])[None]


def body(features_in, gain_outer, bias_outer, w_narrow, gain_inner, bias_inner, w_widen):
    stream = features_in
    rows = stream.shape[1]
    cols = stream.shape[2]
    side = rows * lax.axis_size("row")
    rounds = gain_outer.shape[0] // 4
    row_start = lax.axis_index("row") * rows
    col_start = lax.axis_index("col") * cols
    for repeat in range(rounds):
        stream = averaged_tiles(stream)
        for within in range(4):
            block = repeat * 4 + within
            dilation = 1 + within // 2
            outer_scale = gain_outer[block][:, None, None]
            outer_shift = bias_outer[block][:, None, None]
            inner_scale = gain_inner[block][:, None, None]
            inner_shift = bias_inner[block][:, None, None]
            deep = padded_2(stream, (("row", 1), ("col", 2)), 2 * dilation)
            hidden = jax.nn.relu(deep.astype(jnp.float32) * outer_scale + outer_shift)
            hidden = jnp.where(
                inside_mask(
                    row_start,
                    col_start,
                    2 * dilation,
                    rows + 4 * dilation,
                    cols + 4 * dilation,
                    side,
                ),
                hidden,
                0.0,
            ).astype(jnp.bfloat16)
            narrow = dilated_taps(
                hidden, w_narrow[block], dilation, rows + 2 * dilation, cols + 2 * dilation
            )
            inner = jax.nn.relu(narrow * inner_scale + inner_shift)
            inner = jnp.where(
                inside_mask(
                    row_start, col_start, dilation, rows + 2 * dilation, cols + 2 * dilation, side
                ),
                inner,
                0.0,
            ).astype(jnp.bfloat16)
            widened = dilated_taps(inner, w_widen[block], dilation, rows, cols)
            stream = (stream.astype(jnp.float32) + widened).astype(jnp.bfloat16)
    return stream


def dispatch(mesh, *args):
    channels, rows, width = args[0].shape
    whole_rows = mesh.shape["col"] == 1 and width == rows * mesh.shape["row"]
    packs = LANES % channels == 0 and rows * channels % LANES == 0 and width % LANES == 0
    even = rows % 2 == 0 and rows * rows * channels % (8 * LANES) == 0
    if whole_rows and packs and even:
        return fused_body(*args)
    return body(*args)


def solution(mesh):
    in_specs = (P(None, ("groups", "row"), "col"), P(), P(), P(), P(), P(), P())
    out_specs = P(None, ("groups", "row"), "col")
    return jax.shard_map(
        functools.partial(dispatch, mesh),
        mesh=mesh,
        in_specs=in_specs,
        out_specs=out_specs,
        check_vma=False,
    )
```

```python
import functools

import numpy as np
import jax
import jax.numpy as jnp
from jax import lax
from jax.experimental import pallas as pl
from jax.experimental.pallas import tpu as pltpu
from jax.sharding import PartitionSpec as P

GROUPS = ((1, 1), (2,), (2,))
LANES = 128


def remote(src, dst, send_sem, recv_sem, target):
    return pltpu.make_async_remote_copy(
        src_ref=src,
        dst_ref=dst,
        send_sem=send_sem,
        recv_sem=recv_sem,
        device_id={"row": target},
        device_id_type=pl.DeviceIdType.MESH,
    )


def spread_constants(rows, channels, width):
    count = width // rows
    halves = rows * channels // LANES
    pieces = rows * halves
    subs = LANES // channels
    p = np.arange(width * halves)
    pack = np.zeros((width * halves, halves * width), np.float32)
    pack[p, (p % halves) * width + p // halves] = 1
    o = np.arange(rows * width)
    xx, x = o // width, o % width
    j, r = x // rows, x % rows
    q = (r % subs) * (count * pieces) + j * pieces + xx * halves + r // subs
    unpack = np.zeros((subs * count * pieces, rows * width), np.float32)
    unpack[q, o] = 1
    return jnp.asarray(pack), jnp.asarray(unpack)


def shifted_sum(parts, dilation, lane):
    width = lane.shape[-1]
    low = jnp.where(lane < dilation, 0.0, pltpu.roll(parts[0], dilation, 1))
    high = jnp.where(lane >= width - dilation, 0.0, pltpu.roll(parts[2], width - dilation, 1))
    return parts[1] + low + high


def shifts(value, dilation, lane):
    width = lane.shape[-1]
    low = jnp.where(lane < dilation, 0.0, pltpu.roll(value, dilation, 1))
    high = jnp.where(lane >= width - dilation, 0.0, pltpu.roll(value, width - dilation, 1))
    return low, value, high


def network_kernel(
    count, rounds, x_ref, *refs
):
    channels, rows, width = x_ref.shape
    hbm, out_ref, scratch = refs[:8], refs[8], refs[9:]
    held, held_sem, params_ref, x_wide = scratch[:8], scratch[8], scratch[9], scratch[10]
    scratch = scratch[11:]
    pack_ref, unpack_ref, raw_ref, ww_ref = held[:4]
    blocks, mid = raw_ref.shape[:2]
    fetches = [
        pltpu.make_async_copy(source, target, held_sem.at[i])
        for i, (source, target) in enumerate(zip(hbm, held))
    ]
    for fetch in fetches:
        fetch.start()
    side = rows * count
    halves = rows * channels // LANES
    subs = LANES // channels
    pieces = rows * halves
    groups = len(GROUPS)
    tiles = scratch[:groups]
    sent, got, stream_buf, hidden_buf, inner_buf, wn_ref = scratch[groups:][:6]
    mirror_send, mirror_recv, halo_send, halo_recv = scratch[groups + 6 :]
    me = lax.axis_index("row")

    def wrapped(k):
        t = me + k
        return jnp.where(t >= count, t - count, t)

    barrier = pltpu.get_barrier_semaphore()

    far_first = sorted(range(1, count), key=lambda k: -min(k, count - k))

    def greet(k):
        pl.semaphore_signal(
            barrier,
            inc=1,
            device_id={"row": wrapped(k)},
            device_id_type=pl.DeviceIdType.MESH,
        )

    for k in far_first:
        greet(k)
    for rd, gi in [(rd, gi) for rd in range(rounds) for gi in range(groups)]:
        tile = tiles[gi].at[rd]
        reach = tile.shape[0] // 2
        for k in range(1, reach + 1):
            for sign in (-1, 1):
                slot = reach + sign * k
                other = me + sign * k

                @pl.when((other < 0) | (other >= count))
                def _():
                    tile[slot] = jnp.zeros(tile.shape[1:], tile.dtype)

    def pack(rd, stream):
        flat = [s for s in stream]
        per = LANES // channels
        cat = jnp.concatenate(
            [jnp.concatenate(flat[h * per : (h + 1) * per], axis=0) for h in range(halves)], axis=1
        )
        packed = lax.dot_general(
            pack_ref[...].astype(jnp.bfloat16), cat, (((1,), (1,)), ((), ())), preferred_element_type=jnp.float32
        )
        sent[rd] = packed.reshape(count, pieces, LANES).astype(jnp.bfloat16)

    def mirror_copy(rd, target, source):
        return remote(
            sent.at[rd, target],
            got.at[rd, source],
            mirror_send.at[rd],
            mirror_recv.at[rd],
            target,
        )

    def mirror_all(rd):
        rest = pl.ds(0, count - 1)
        return remote(
            sent.at[rd, rest],
            got.at[rd, rest],
            mirror_send.at[rd],
            mirror_recv.at[rd],
            wrapped(1),
        )

    lane = lax.broadcasted_iota(jnp.int32, (1, width), 1)
    x_wide[...] = x_ref[...].astype(jnp.float32)
    stream = [x_wide[:, r, :].astype(jnp.bfloat16) for r in range(rows)]
    fetches[0].wait()
    pl.semaphore_wait(barrier, count - 1)
    for r in range(rows):
        stream_buf[r] = stream[r]

    def one_round(rd, carry):
        stream = [stream_buf[r] for r in range(rows)]
        pack(rd, stream)
        for k in far_first:
            mirror_copy(rd, wrapped(k), me).start()
        got[rd, me] = sent[rd, me]

        @pl.when(rd == 0)
        def _():
            for fetch in fetches[1:]:
                fetch.wait()
            outer = jnp.concatenate([held[4][...], held[5][...]], axis=1)
            inner = jnp.concatenate([held[6][...], held[7][...]], axis=1)
            columns = jnp.concatenate([outer.T, inner.T], axis=0)
            for b in range(blocks):
                params_ref[b] = jnp.broadcast_to(columns[:, b : b + 1], params_ref.shape[1:])

            def reorder(b, carry):
                raw = raw_ref[b]
                for kx in range(3):
                    taps = [(3 * ky + kx) * channels for ky in range(3)]
                    wn_ref[b, kx * mid : (kx + 1) * mid] = jnp.concatenate(
                        [raw[:, t : t + channels] for t in taps], axis=1
                    )
                return carry

            lax.fori_loop(0, blocks, reorder, 0)
        mirror_all(rd).wait_recv()

        arrived = got[rd].astype(jnp.float32).reshape(count * pieces, LANES).T
        arrived = jnp.concatenate(
            [arrived[u * channels : (u + 1) * channels] for u in range(subs)], axis=1
        ).astype(jnp.bfloat16)
        partner = jnp.dot(
            arrived, unpack_ref[...].astype(jnp.bfloat16), preferred_element_type=jnp.float32
        )
        stream = [
            (
                (stream[r].astype(jnp.float32) + partner[:, r * width : (r + 1) * width]) * 0.5
            ).astype(jnp.bfloat16)
            for r in range(rows)
        ]

        block = rd * sum(len(g) for g in GROUPS)
        for gi, group in enumerate(GROUPS):
            phase = rd * groups + gi
            tile = tiles[gi].at[rd]
            reach = tile.shape[0] // 2
            for r in range(rows):
                tile[reach, r] = stream[r]

            def halo_copy(k, slot_there, target):
                return remote(
                    tile.at[reach],
                    tile.at[slot_there],
                    halo_send.at[phase, reach + k],
                    halo_recv.at[phase, slot_there],
                    target,
                )

            offsets = [s * k for k in range(1, reach + 1) for s in (-1, 1)]
            for k in offsets:

                @pl.when((me + k >= 0) & (me + k < count))
                def _():
                    halo_copy(k, reach - k, me + k).start()

            halo = 2 * sum(group)
            lo = reach * rows - halo
            hi = (reach + 1) * rows + halo
            first_row = (me - reach) * rows

            def inside(e):
                g = first_row + e
                return jnp.where((g >= 0) & (g < side), 1.0, 0.0).astype(jnp.float32)

            def masked(value, e):
                if reach * rows <= e < (reach + 1) * rows:
                    return value
                return value * inside(e)

            for bi, d in enumerate(group):

                def param(start, size):
                    return params_ref[block, start : start + size]

                scale_o = param(0, channels)
                shift_o = param(channels, channels)
                scale_i = param(2 * channels, mid)
                shift_i = param(2 * channels + mid, mid)

                def load(e):
                    return tile[e // rows, e % rows] if bi == 0 else stream_buf[e]

                own = range(reach * rows, (reach + 1) * rows)
                outer = [e for e in range(lo, hi) if e not in own]
                for part in (own, outer):
                    if part is outer and bi == 0:
                        for k in offsets:

                            @pl.when((me + k >= 0) & (me + k < count))
                            def _():
                                halo_copy(k, reach + k, me + k).wait_recv()

                    for e in part:
                        value = jnp.maximum(load(e).astype(jnp.float32) * scale_o + shift_o, 0.0)
                        hidden_buf[e] = masked(value, e).astype(jnp.bfloat16)
                for e, some in [(lo + d, hi - lo - 2 * d)]:
                    both = jnp.concatenate(
                        [
                            jnp.concatenate([hidden_buf[e + i + (ky - 1) * d] for ky in range(3)], axis=0)
                            for i in range(some)
                        ],
                        axis=1,
                    )
                    y = jnp.dot(wn_ref[block], both, preferred_element_type=jnp.float32)
                    for i in range(some):
                        parts = [
                            y[kx * mid : (kx + 1) * mid, i * width : (i + 1) * width]
                            for kx in range(3)
                        ]
                        narrow = shifted_sum(parts, d, lane)
                        value = jnp.maximum(narrow * scale_i + shift_i, 0.0)
                        value = masked(value, e + i)
                        for kx, part in enumerate(shifts(value, d, lane)):
                            inner_buf[e + i, kx * mid : (kx + 1) * mid] = part.astype(jnp.bfloat16)
                lo, hi = lo + 2 * d, hi - 2 * d
                final = bi == len(group) - 1
                stream = [None] * rows
                for e, some in [(lo, hi - lo)]:
                    both = jnp.concatenate(
                        [
                            jnp.concatenate([inner_buf[e + i + (ky - 1) * d] for ky in range(3)], axis=0)
                            for i in range(some)
                        ],
                        axis=1,
                    )
                    y = jnp.dot(ww_ref[block], both, preferred_element_type=jnp.float32)
                    for i in range(some):
                        widened = y[:, i * width : (i + 1) * width]
                        value = (load(e + i).astype(jnp.float32) + widened).astype(jnp.bfloat16)
                        if final:
                            stream[e + i - lo] = value
                        else:
                            stream_buf[e + i] = value
                block += 1
        for r in range(rows):
            stream_buf[r] = stream[r]
        return carry

    lax.fori_loop(0, rounds, one_round, 0)
    for r in range(rows):
        out_ref[r] = stream_buf[r]

    for rd in range(rounds):
        mirror_all(rd).wait_send()
        for gi in range(groups):
            phase = rd * groups + gi
            tile = tiles[gi].at[rd]
            reach = tile.shape[0] // 2
            for k in [s * k for k in range(1, reach + 1) for s in (-1, 1)]:

                @pl.when((me + k >= 0) & (me + k < count))
                def _():
                    remote(
                        tile.at[reach],
                        tile.at[reach - k],
                        halo_send.at[phase, reach + k],
                        halo_recv.at[phase, reach - k],
                        me + k,
                    ).wait_send()


def fused_body(features_in, gain_outer, bias_outer, w_narrow, gain_inner, bias_inner, w_widen):
    channels, rows, width = features_in.shape
    blocks, mid = gain_inner.shape
    count = lax.axis_size("row")
    rounds = blocks // sum(len(g) for g in GROUPS)
    halves = rows * channels // LANES
    pack, unpack = spread_constants(rows, channels, width)
    fetched = (pack, unpack, w_narrow, w_widen, gain_outer, bias_outer, gain_inner, bias_inner)
    reaches = [-(-2 * sum(g) // rows) for g in GROUPS]
    tall = (2 * max(reaches) + 1) * rows
    phases = rounds * len(GROUPS)
    dma = pltpu.SemaphoreType.DMA
    out = pl.pallas_call(
        functools.partial(network_kernel, count, rounds),
        out_shape=jax.ShapeDtypeStruct((rows, channels, width), jnp.bfloat16),
        in_specs=[pl.BlockSpec(memory_space=pltpu.VMEM)]
        + [pl.BlockSpec(memory_space=pltpu.HBM)] * len(fetched),
        out_specs=pl.BlockSpec(memory_space=pltpu.VMEM),
        scratch_shapes=[pltpu.VMEM(a.shape, a.dtype) for a in fetched]
        + [dma((len(fetched),)), pltpu.VMEM((blocks, 2 * (channels + mid), width), jnp.float32)]
        + [pltpu.VMEM(features_in.shape, jnp.float32)]
        + [
            pltpu.VMEM((rounds, 2 * r + 1, rows, channels, width), jnp.bfloat16)
            for r in reaches
        ]
        + [
            pltpu.VMEM((rounds, count, rows * halves, LANES), jnp.bfloat16),
            pltpu.VMEM((rounds, count, rows * halves, LANES), jnp.bfloat16),
            pltpu.VMEM((tall, channels, width), jnp.bfloat16),
            pltpu.VMEM((tall, channels, width), jnp.bfloat16),
            pltpu.VMEM((tall, 3 * mid, width), jnp.bfloat16),
            pltpu.VMEM((blocks, 3 * mid, 3 * channels), jnp.bfloat16),
            dma((rounds,)),
            dma((rounds,)),
            dma((phases, 2 * max(reaches) + 1)),
            dma((phases, 2 * max(reaches) + 1)),
        ],
        compiler_params=pltpu.CompilerParams(
            collective_id=0, has_side_effects=True, vmem_limit_bytes=60 * 1024 * 1024
        ),
    )(
        features_in,
        *fetched,
    )
    return out.transpose(1, 0, 2)


def padded_2(block, sides, width):
    for axis, dim in sides:
        count = lax.axis_size(axis)
        forward = [(i, i + 1) for i in range(count - 1)]
        backward = [(target, source) for source, target in forward]
        low = lax.ppermute(
            lax.slice_in_dim(block, block.shape[dim] - width, None, axis=dim), axis, forward
        )
        high = lax.ppermute(lax.slice_in_dim(block, 0, width, axis=dim), axis, backward)
        block = jnp.concatenate([low, block, high], axis=dim)
    return block


def dilated_taps(padded, weight, dilation, rows, cols):
    channels = padded.shape[0]
    total = None
    for vertical in range(3):
        for lateral in range(3):
            tap_index = vertical * 3 + lateral
            window = padded[
                :,
                vertical * dilation : vertical * dilation + rows,
                lateral * dilation : lateral * dilation + cols,
            ]
            weight_tap = weight[:, tap_index * channels : (tap_index + 1) * channels]
            term = jnp.einsum("oc,crw->orw", weight_tap, window, preferred_element_type=jnp.float32)
            total = term if total is None else total + term
    return total


def mirrored(stream):
    channels = stream.shape[0]
    rows = stream.shape[1]
    width = stream.shape[2]
    row_count = lax.axis_size("row")
    core_count = lax.axis_size("col")
    squares = stream.reshape(channels, rows, row_count, core_count, rows)
    outgoing = squares.transpose(3, 2, 4, 1, 0).reshape(
        core_count, row_count, rows * rows * channels
    )
    received = lax.all_to_all(
        lax.all_to_all(outgoing, "row", split_axis=1, concat_axis=1, tiled=True),
        "col",
        split_axis=0,
        concat_axis=0,
        tiled=True,
    )
    partner = (
        received.reshape(core_count, row_count, rows, rows, channels)
        .transpose(4, 2, 1, 0, 3)
        .reshape(channels, rows, width)
    )
    return ((stream.astype(jnp.float32) + partner.astype(jnp.float32)) * 0.5).astype(jnp.bfloat16)


def averaged_tiles(stream):
    strips = lax.all_to_all(stream, "col", split_axis=1, concat_axis=2, tiled=True)
    merged = mirrored(strips)
    return lax.all_to_all(merged, "col", split_axis=2, concat_axis=1, tiled=True)


def inside_mask(row_start, col_start, offset, row_count, col_count, side):
    global_rows = row_start - offset + lax.iota(jnp.int32, row_count)
    global_cols = col_start - offset + lax.iota(jnp.int32, col_count)
    rows_ok = (global_rows >= 0) & (global_rows < side)
    cols_ok = (global_cols >= 0) & (global_cols < side)
    return (rows_ok[:, None] & cols_ok[None, :])[None]


def body(features_in, gain_outer, bias_outer, w_narrow, gain_inner, bias_inner, w_widen):
    stream = features_in
    rows = stream.shape[1]
    cols = stream.shape[2]
    side = rows * lax.axis_size("row")
    rounds = gain_outer.shape[0] // 4
    row_start = lax.axis_index("row") * rows
    col_start = lax.axis_index("col") * cols
    for repeat in range(rounds):
        stream = averaged_tiles(stream)
        for within in range(4):
            block = repeat * 4 + within
            dilation = 1 + within // 2
            outer_scale = gain_outer[block][:, None, None]
            outer_shift = bias_outer[block][:, None, None]
            inner_scale = gain_inner[block][:, None, None]
            inner_shift = bias_inner[block][:, None, None]
            deep = padded_2(stream, (("row", 1), ("col", 2)), 2 * dilation)
            hidden = jax.nn.relu(deep.astype(jnp.float32) * outer_scale + outer_shift)
            hidden = jnp.where(
                inside_mask(
                    row_start,
                    col_start,
                    2 * dilation,
                    rows + 4 * dilation,
                    cols + 4 * dilation,
                    side,
                ),
                hidden,
                0.0,
            ).astype(jnp.bfloat16)
            narrow = dilated_taps(
                hidden, w_narrow[block], dilation, rows + 2 * dilation, cols + 2 * dilation
            )
            inner = jax.nn.relu(narrow * inner_scale + inner_shift)
            inner = jnp.where(
                inside_mask(
                    row_start, col_start, dilation, rows + 2 * dilation, cols + 2 * dilation, side
                ),
                inner,
                0.0,
            ).astype(jnp.bfloat16)
            widened = dilated_taps(inner, w_widen[block], dilation, rows, cols)
            stream = (stream.astype(jnp.float32) + widened).astype(jnp.bfloat16)
    return stream


def dispatch(mesh, *args):
    channels, rows, width = args[0].shape
    whole_rows = mesh.shape["col"] == 1 and width == rows * mesh.shape["row"]
    packs = LANES % channels == 0 and rows * channels % LANES == 0 and width % LANES == 0
    even = rows % 2 == 0 and rows * rows * channels % (8 * LANES) == 0
    if whole_rows and packs and even:
        return fused_body(*args)
    return body(*args)


def solution(mesh):
    in_specs = (P(None, ("groups", "row"), "col"), P(), P(), P(), P(), P(), P())
    out_specs = P(None, ("groups", "row"), "col")
    return jax.shard_map(
        functools.partial(dispatch, mesh),
        mesh=mesh,
        in_specs=in_specs,
        out_specs=out_specs,
        check_vma=False,
    )
```

```python
import functools

import numpy as np
import jax
import jax.numpy as jnp
from jax import lax
from jax.experimental import pallas as pl
from jax.experimental.pallas import tpu as pltpu
from jax.sharding import PartitionSpec as P

GROUPS = ((1, 1), (2, 2))
LANES = 128


def remote(src, dst, send_sem, recv_sem, target):
    return pltpu.make_async_remote_copy(
        src_ref=src,
        dst_ref=dst,
        send_sem=send_sem,
        recv_sem=recv_sem,
        device_id={"row": target},
        device_id_type=pl.DeviceIdType.MESH,
    )


def spread_constants(rows, channels, width):
    count = width // rows
    halves = rows * channels // LANES
    pieces = rows * halves
    subs = LANES // channels
    p = np.arange(width * halves)
    pack = np.zeros((width * halves, halves * width), np.float32)
    pack[p, (p % halves) * width + p // halves] = 1
    o = np.arange(rows * width)
    xx, x = o // width, o % width
    j, r = x // rows, x % rows
    q = (r % subs) * (count * pieces) + j * pieces + xx * halves + r // subs
    unpack = np.zeros((subs * count * pieces, rows * width), np.float32)
    unpack[q, o] = 1
    return jnp.asarray(pack), jnp.asarray(unpack)


def shifted_sum(parts, dilation, lane):
    width = lane.shape[-1]
    low = jnp.where(lane < dilation, 0.0, pltpu.roll(parts[0], dilation, 1))
    high = jnp.where(lane >= width - dilation, 0.0, pltpu.roll(parts[2], width - dilation, 1))
    return parts[1] + low + high


def shifts(value, dilation, lane):
    width = lane.shape[-1]
    low = jnp.where(lane < dilation, 0.0, pltpu.roll(value, dilation, 1))
    high = jnp.where(lane >= width - dilation, 0.0, pltpu.roll(value, width - dilation, 1))
    return low, value, high


def network_kernel(
    count, rounds, x_ref, *refs
):
    channels, rows, width = x_ref.shape
    hbm, out_ref, scratch = refs[:8], refs[8], refs[9:]
    held, held_sem, params_ref, x_wide = scratch[:8], scratch[8], scratch[9], scratch[10]
    scratch = scratch[11:]
    pack_ref, unpack_ref, raw_ref, ww_ref = held[:4]
    blocks, mid = raw_ref.shape[:2]
    fetches = [
        pltpu.make_async_copy(source, target, held_sem.at[i])
        for i, (source, target) in enumerate(zip(hbm, held))
    ]
    for fetch in fetches:
        fetch.start()
    side = rows * count
    halves = rows * channels // LANES
    subs = LANES // channels
    pieces = rows * halves
    groups = len(GROUPS)
    tiles = scratch[: rounds * groups]
    sent, got, stream_buf, hidden_buf, inner_buf, wn_ref = scratch[rounds * groups :][:6]
    mirror_send, mirror_recv, halo_send, halo_recv = scratch[rounds * groups + 6 :]
    me = lax.axis_index("row")

    def wrapped(k):
        t = me + k
        return jnp.where(t >= count, t - count, t)

    barrier = pltpu.get_barrier_semaphore()

    far_first = sorted(range(1, count), key=lambda k: -min(k, count - k))

    def greet(k):
        pl.semaphore_signal(
            barrier,
            inc=1,
            device_id={"row": wrapped(k)},
            device_id_type=pl.DeviceIdType.MESH,
        )

    for k in far_first:
        greet(k)
    for phase in range(rounds * groups):
        tile = tiles[phase]
        reach = tile.shape[0] // 2
        for k in range(1, reach + 1):
            for sign in (-1, 1):
                slot = reach + sign * k
                other = me + sign * k

                @pl.when((other < 0) | (other >= count))
                def _():
                    tile[slot] = jnp.zeros(tile.shape[1:], tile.dtype)

    def pack(rd, stream):
        flat = [s for s in stream]
        per = LANES // channels
        cat = jnp.concatenate(
            [jnp.concatenate(flat[h * per : (h + 1) * per], axis=0) for h in range(halves)], axis=1
        )
        packed = lax.dot_general(
            pack_ref[...].astype(jnp.bfloat16), cat, (((1,), (1,)), ((), ())), preferred_element_type=jnp.float32
        )
        sent[rd] = packed.reshape(count, pieces, LANES).astype(jnp.bfloat16)

    def mirror_copy(rd, target, source):
        return remote(
            sent.at[rd, target],
            got.at[rd, source],
            mirror_send.at[rd],
            mirror_recv.at[rd],
            target,
        )

    def mirror_all(rd):
        rest = pl.ds(0, count - 1)
        return remote(
            sent.at[rd, rest],
            got.at[rd, rest],
            mirror_send.at[rd],
            mirror_recv.at[rd],
            wrapped(1),
        )

    lane = lax.broadcasted_iota(jnp.int32, (1, width), 1)
    x_wide[...] = x_ref[...].astype(jnp.float32)
    stream = [x_wide[:, r, :].astype(jnp.bfloat16) for r in range(rows)]
    fetches[0].wait()
    pack(0, stream)
    pl.semaphore_wait(barrier, count - 1)

    for rd in range(rounds):
        if rd:
            pack(rd, stream)

        for k in far_first:
            mirror_copy(rd, wrapped(k), me).start()
        got[rd, me] = sent[rd, me]
        if rd == 0:
            for fetch in fetches[1:]:
                fetch.wait()
            outer = jnp.concatenate([held[4][...], held[5][...]], axis=1)
            inner = jnp.concatenate([held[6][...], held[7][...]], axis=1)
            params_ref[: 2 * channels] = outer.T
            params_ref[2 * channels :] = inner.T

            def reorder(b, carry):
                raw = raw_ref[b]
                for kx in range(3):
                    taps = [(3 * ky + kx) * channels for ky in range(3)]
                    wn_ref[b, kx * mid : (kx + 1) * mid] = jnp.concatenate(
                        [raw[:, t : t + channels] for t in taps], axis=1
                    )
                return carry

            lax.fori_loop(0, blocks, reorder, 0)
        mirror_all(rd).wait_recv()

        arrived = got[rd].astype(jnp.float32).reshape(count * pieces, LANES).T
        arrived = jnp.concatenate(
            [arrived[u * channels : (u + 1) * channels] for u in range(subs)], axis=1
        ).astype(jnp.bfloat16)
        partner = jnp.dot(
            arrived, unpack_ref[...].astype(jnp.bfloat16), preferred_element_type=jnp.float32
        )
        stream = [
            (
                (stream[r].astype(jnp.float32) + partner[:, r * width : (r + 1) * width]) * 0.5
            ).astype(jnp.bfloat16)
            for r in range(rows)
        ]

        block = rd * sum(len(g) for g in GROUPS)
        for gi, group in enumerate(GROUPS):
            phase = rd * groups + gi
            tile = tiles[phase]
            reach = tile.shape[0] // 2
            for r in range(rows):
                tile[reach, r] = stream[r]

            def halo_copy(k, slot_there, target):
                return remote(
                    tile.at[reach],
                    tile.at[slot_there],
                    halo_send.at[phase, reach + k],
                    halo_recv.at[phase, slot_there],
                    target,
                )

            offsets = [s * k for k in range(1, reach + 1) for s in (-1, 1)]
            for k in offsets:

                @pl.when((me + k >= 0) & (me + k < count))
                def _():
                    halo_copy(k, reach - k, me + k).start()

            halo = 2 * sum(group)
            lo = reach * rows - halo
            hi = (reach + 1) * rows + halo
            first_row = (me - reach) * rows

            def inside(e):
                g = first_row + e
                return jnp.where((g >= 0) & (g < side), 1.0, 0.0).astype(jnp.float32)

            def masked(value, e):
                if reach * rows <= e < (reach + 1) * rows:
                    return value
                return value * inside(e)

            for bi, d in enumerate(group):

                def param(start, size):
                    return jnp.broadcast_to(
                        params_ref[start : start + size, block : block + 1], (size, width)
                    )

                scale_o = param(0, channels)
                shift_o = param(channels, channels)
                scale_i = param(2 * channels, mid)
                shift_i = param(2 * channels + mid, mid)

                def load(e):
                    return tile[e // rows, e % rows] if bi == 0 else stream_buf[e]

                for far in range(reach + 1):
                    part = [
                        e for e in range(lo, hi) if abs(e // rows - reach) == far
                    ]
                    if far and bi == 0:
                        for k in (-far, far):

                            @pl.when((me + k >= 0) & (me + k < count))
                            def _():
                                halo_copy(k, reach + k, me + k).wait_recv()

                    for e in part:
                        value = jnp.maximum(load(e).astype(jnp.float32) * scale_o + shift_o, 0.0)
                        hidden_buf[e] = masked(value, e).astype(jnp.bfloat16)
                for e, some in [(lo + d, hi - lo - 2 * d)]:
                    both = jnp.concatenate(
                        [
                            jnp.concatenate([hidden_buf[e + i + (ky - 1) * d] for ky in range(3)], axis=0)
                            for i in range(some)
                        ],
                        axis=1,
                    )
                    y = jnp.dot(wn_ref[block], both, preferred_element_type=jnp.float32)
                    for i in range(some):
                        parts = [
                            y[kx * mid : (kx + 1) * mid, i * width : (i + 1) * width]
                            for kx in range(3)
                        ]
                        narrow = shifted_sum(parts, d, lane)
                        value = jnp.maximum(narrow * scale_i + shift_i, 0.0)
                        value = masked(value, e + i)
                        for kx, part in enumerate(shifts(value, d, lane)):
                            inner_buf[e + i, kx * mid : (kx + 1) * mid] = part.astype(jnp.bfloat16)
                lo, hi = lo + 2 * d, hi - 2 * d
                final = bi == len(group) - 1
                stream = [None] * rows
                for e, some in [(lo, hi - lo)]:
                    both = jnp.concatenate(
                        [
                            jnp.concatenate([inner_buf[e + i + (ky - 1) * d] for ky in range(3)], axis=0)
                            for i in range(some)
                        ],
                        axis=1,
                    )
                    y = jnp.dot(ww_ref[block], both, preferred_element_type=jnp.float32)
                    for i in range(some):
                        widened = y[:, i * width : (i + 1) * width]
                        value = (load(e + i).astype(jnp.float32) + widened).astype(jnp.bfloat16)
                        if final:
                            stream[e + i - lo] = value
                        else:
                            stream_buf[e + i] = value
                block += 1

    for r in range(rows):
        out_ref[r] = stream[r]

    for rd in range(rounds):
        mirror_all(rd).wait_send()
        for gi in range(groups):
            phase = rd * groups + gi
            tile = tiles[phase]
            reach = tile.shape[0] // 2
            for k in [s * k for k in range(1, reach + 1) for s in (-1, 1)]:

                @pl.when((me + k >= 0) & (me + k < count))
                def _():
                    remote(
                        tile.at[reach],
                        tile.at[reach - k],
                        halo_send.at[phase, reach + k],
                        halo_recv.at[phase, reach - k],
                        me + k,
                    ).wait_send()


def fused_body(features_in, gain_outer, bias_outer, w_narrow, gain_inner, bias_inner, w_widen):
    channels, rows, width = features_in.shape
    blocks, mid = gain_inner.shape
    count = lax.axis_size("row")
    rounds = blocks // sum(len(g) for g in GROUPS)
    halves = rows * channels // LANES
    pack, unpack = spread_constants(rows, channels, width)
    fetched = (pack, unpack, w_narrow, w_widen, gain_outer, bias_outer, gain_inner, bias_inner)
    reaches = [-(-2 * sum(g) // rows) for g in GROUPS]
    tall = (2 * max(reaches) + 1) * rows
    phases = rounds * len(GROUPS)
    dma = pltpu.SemaphoreType.DMA
    out = pl.pallas_call(
        functools.partial(network_kernel, count, rounds),
        out_shape=jax.ShapeDtypeStruct((rows, channels, width), jnp.bfloat16),
        in_specs=[pl.BlockSpec(memory_space=pltpu.VMEM)]
        + [pl.BlockSpec(memory_space=pltpu.HBM)] * len(fetched),
        out_specs=pl.BlockSpec(memory_space=pltpu.VMEM),
        scratch_shapes=[pltpu.VMEM(a.shape, a.dtype) for a in fetched]
        + [dma((len(fetched),)), pltpu.VMEM((2 * (channels + mid), blocks), jnp.float32)]
        + [pltpu.VMEM(features_in.shape, jnp.float32)]
        + [
            pltpu.VMEM((2 * r + 1, rows, channels, width), jnp.bfloat16)
            for _ in range(rounds)
            for r in reaches
        ]
        + [
            pltpu.VMEM((rounds, count, rows * halves, LANES), jnp.bfloat16),
            pltpu.VMEM((rounds, count, rows * halves, LANES), jnp.bfloat16),
            pltpu.VMEM((tall, channels, width), jnp.bfloat16),
            pltpu.VMEM((tall, channels, width), jnp.bfloat16),
            pltpu.VMEM((tall, 3 * mid, width), jnp.bfloat16),
            pltpu.VMEM((blocks, 3 * mid, 3 * channels), jnp.bfloat16),
            dma((rounds,)),
            dma((rounds,)),
            dma((phases, 2 * max(reaches) + 1)),
            dma((phases, 2 * max(reaches) + 1)),
        ],
        compiler_params=pltpu.CompilerParams(
            collective_id=0, has_side_effects=True, vmem_limit_bytes=60 * 1024 * 1024
        ),
    )(
        features_in,
        *fetched,
    )
    return out.transpose(1, 0, 2)


def padded_2(block, sides, width):
    for axis, dim in sides:
        count = lax.axis_size(axis)
        forward = [(i, i + 1) for i in range(count - 1)]
        backward = [(target, source) for source, target in forward]
        low = lax.ppermute(
            lax.slice_in_dim(block, block.shape[dim] - width, None, axis=dim), axis, forward
        )
        high = lax.ppermute(lax.slice_in_dim(block, 0, width, axis=dim), axis, backward)
        block = jnp.concatenate([low, block, high], axis=dim)
    return block


def dilated_taps(padded, weight, dilation, rows, cols):
    channels = padded.shape[0]
    total = None
    for vertical in range(3):
        for lateral in range(3):
            tap_index = vertical * 3 + lateral
            window = padded[
                :,
                vertical * dilation : vertical * dilation + rows,
                lateral * dilation : lateral * dilation + cols,
            ]
            weight_tap = weight[:, tap_index * channels : (tap_index + 1) * channels]
            term = jnp.einsum("oc,crw->orw", weight_tap, window, preferred_element_type=jnp.float32)
            total = term if total is None else total + term
    return total


def mirrored(stream):
    channels = stream.shape[0]
    rows = stream.shape[1]
    width = stream.shape[2]
    row_count = lax.axis_size("row")
    core_count = lax.axis_size("col")
    squares = stream.reshape(channels, rows, row_count, core_count, rows)
    outgoing = squares.transpose(3, 2, 4, 1, 0).reshape(
        core_count, row_count, rows * rows * channels
    )
    received = lax.all_to_all(
        lax.all_to_all(outgoing, "row", split_axis=1, concat_axis=1, tiled=True),
        "col",
        split_axis=0,
        concat_axis=0,
        tiled=True,
    )
    partner = (
        received.reshape(core_count, row_count, rows, rows, channels)
        .transpose(4, 2, 1, 0, 3)
        .reshape(channels, rows, width)
    )
    return ((stream.astype(jnp.float32) + partner.astype(jnp.float32)) * 0.5).astype(jnp.bfloat16)


def averaged_tiles(stream):
    strips = lax.all_to_all(stream, "col", split_axis=1, concat_axis=2, tiled=True)
    merged = mirrored(strips)
    return lax.all_to_all(merged, "col", split_axis=2, concat_axis=1, tiled=True)


def inside_mask(row_start, col_start, offset, row_count, col_count, side):
    global_rows = row_start - offset + lax.iota(jnp.int32, row_count)
    global_cols = col_start - offset + lax.iota(jnp.int32, col_count)
    rows_ok = (global_rows >= 0) & (global_rows < side)
    cols_ok = (global_cols >= 0) & (global_cols < side)
    return (rows_ok[:, None] & cols_ok[None, :])[None]


def body(features_in, gain_outer, bias_outer, w_narrow, gain_inner, bias_inner, w_widen):
    stream = features_in
    rows = stream.shape[1]
    cols = stream.shape[2]
    side = rows * lax.axis_size("row")
    rounds = gain_outer.shape[0] // 4
    row_start = lax.axis_index("row") * rows
    col_start = lax.axis_index("col") * cols
    for repeat in range(rounds):
        stream = averaged_tiles(stream)
        for within in range(4):
            block = repeat * 4 + within
            dilation = 1 + within // 2
            outer_scale = gain_outer[block][:, None, None]
            outer_shift = bias_outer[block][:, None, None]
            inner_scale = gain_inner[block][:, None, None]
            inner_shift = bias_inner[block][:, None, None]
            deep = padded_2(stream, (("row", 1), ("col", 2)), 2 * dilation)
            hidden = jax.nn.relu(deep.astype(jnp.float32) * outer_scale + outer_shift)
            hidden = jnp.where(
                inside_mask(
                    row_start,
                    col_start,
                    2 * dilation,
                    rows + 4 * dilation,
                    cols + 4 * dilation,
                    side,
                ),
                hidden,
                0.0,
            ).astype(jnp.bfloat16)
            narrow = dilated_taps(
                hidden, w_narrow[block], dilation, rows + 2 * dilation, cols + 2 * dilation
            )
            inner = jax.nn.relu(narrow * inner_scale + inner_shift)
            inner = jnp.where(
                inside_mask(
                    row_start, col_start, dilation, rows + 2 * dilation, cols + 2 * dilation, side
                ),
                inner,
                0.0,
            ).astype(jnp.bfloat16)
            widened = dilated_taps(inner, w_widen[block], dilation, rows, cols)
            stream = (stream.astype(jnp.float32) + widened).astype(jnp.bfloat16)
    return stream


def dispatch(mesh, *args):
    channels, rows, width = args[0].shape
    whole_rows = mesh.shape["col"] == 1 and width == rows * mesh.shape["row"]
    packs = LANES % channels == 0 and rows * channels % LANES == 0 and width % LANES == 0
    even = rows % 2 == 0 and rows * rows * channels % (8 * LANES) == 0
    if whole_rows and packs and even:
        return fused_body(*args)
    return body(*args)


def solution(mesh):
    in_specs = (P(None, ("groups", "row"), "col"), P(), P(), P(), P(), P(), P())
    out_specs = P(None, ("groups", "row"), "col")
    return jax.shard_map(
        functools.partial(dispatch, mesh),
        mesh=mesh,
        in_specs=in_specs,
        out_specs=out_specs,
        check_vma=False,
    )
```
